256 devices in a mesh: seg: 32 (over y, x, core), fe: 8 (over z).
Axes of the slice: x: 4, y: 4, z: 8, core: 2. Of those that a mesh axis runs over, the one named last changes fastest.
Arguments:
- seg_pos: float32 [3, 4096], P(None, 'seg'), may hold values from 0 to 1
- burgers: float32 [3, 4096], P(None, 'seg'), may hold values from -6 to 6
- seg_tile: int32 [4096], P('seg'), may hold values from 0 to 7
- quad_pos: float32 [3, 524288], P(None, 'fe'), may hold values from 0 to 1
- quad_node: int32 [524288], P('fe'), may hold values from 0 to 65535
- stiffness: float32 [128, 128, 1024], P('seg', None, 'fe'), may hold values from 0.05 to 2
Outputs:
- correction: float32 [3, 128, 128, 1024], P(None, 'seg', None, 'fe')
- stress: float32 [3, 4096], P(None, 'seg')
The draws below stay inside these ranges and needn't reach their ends.
Inputs may be any that keep to these rules, and one draw needn't show every extreme that they name: `quad_node`: entry q numbers a node of the block of 4 x 128 x 128 nodes whose corner is grid node ((q mod 65536) // 2048 * 4, 0, q // 65536 * 128), first index slowest.
All inputs are finite; a program needn't handle non-finite values.
Results may differ from the reference program's by a relative error of at most 0.0003.
Values sent between devices are 32-bit elements; how exact they have to be, the bound alone decides.
No kernel may reach another device: no remote copies, remote signals or barrier semaphores. Data moves between devices by JAX's collectives and lax.ppermute only.
A program may use at most 128 MiB of HBM per device.

```python
import math
import jax
import jax.numpy as jnp
from jax import lax

Q_DEV = 2048
CX = 4
NY = 128
CZ = 128
ITERS = 2
SEGS = 4096
QB = 65536
QPTS = 524288
NX = 128
NZ = 1024
N_FE = 8


def with_ends(result, own_key, low, top_value):
    longest = result.shape.index(max(result.shape))
    spots = []
    for shift in (0, 1):
        where = [jax.random.randint(jax.random.fold_in(own_key, axis), (), 0, length) for axis, length in enumerate(result.shape)]
        where[longest] = (where[longest] + shift) % result.shape[longest]
        spots.append(tuple(where))
    return result.at[spots[0]].set(low).at[spots[1]].set(top_value)


def levels(rng, shape, cuts, least, high):
    loudness = 1.0
    for axis_at, shards_of in cuts:
        heights = jax.random.uniform(jax.random.fold_in(jax.random.fold_in(rng, 6), axis_at), (shards_of,), jnp.float32, least / len(cuts), high / len(cuts))
        loudness = loudness * jnp.repeat(jnp.exp(heights), shape[axis_at] // shards_of).reshape((-1,) + (1,) * (len(shape) - 1 - axis_at))
    return loudness


def normal_values(own_key, dims, deviation, reach, shards=(), kind=jnp.bfloat16):
    gain = levels(own_key, dims, shards, -0.22, 0.18) if shards else 1.0
    values = jax.random.normal(own_key, dims, jnp.float32) * deviation * gain
    return jnp.minimum(jnp.maximum(values, -reach), reach).astype(kind)


def setup_inputs(seed: int = 0) -> dict:
    keys = jax.random.split(jax.random.key(seed), 7)
    return {
        "seg_pos": jnp.clip(1.0 * jax.random.uniform(keys[0], (3, SEGS), jnp.float32) ** levels(keys[0], (3, SEGS), ((1, 32),), -0.2, 0.2), 0.0, 1.0),
        "burgers": normal_values(keys[1], (3, SEGS), 1.0, 6.0, ((1, 32),), jnp.float32),
        "seg_tile": with_ends(jax.random.randint(keys[2], (SEGS,), 0, N_FE), jax.random.fold_in(keys[2], 1), 0, N_FE - 1).astype(jnp.int32),
        "quad_pos": jnp.clip(1.0 * jax.random.uniform(keys[3], (3, QPTS), jnp.float32) ** levels(keys[3], (3, QPTS), ((1, 8),), -0.2, 0.2), 0.0, 1.0),
        "quad_node": with_ends(jax.random.randint(keys[4], (QPTS,), 0, CX * NY * CZ), jax.random.fold_in(keys[4], 1), 0, (CX * NY * CZ) - 1).astype(jnp.int32),
        "stiffness": jnp.clip(jnp.exp(math.log(2.0) - 3.6888794 * jax.random.uniform(keys[5], (NX, NY, NZ), jnp.float32) ** levels(keys[5], (NX, NY, NZ), ((0, 32), (2, 8)), -0.2, 0.2)), 0.05, 2.0),
    }


CORE = 0.0001
STRENGTH = 0.001
HIGH = lax.Precision.HIGHEST

def near_weights(q_pos, q_tile, s_pos, s_tile):
    dist = (q_pos[0][:, None] - s_pos[0][None, :]) ** 2
    dist = dist + (q_pos[1][:, None] - s_pos[1][None, :]) ** 2
    dist = dist + (q_pos[2][:, None] - s_pos[2][None, :]) ** 2
    inverse = lax.rsqrt(dist + CORE)
    near = jnp.abs(q_tile[:, None] - s_tile[None, :]) <= 1
    return jnp.where(near, STRENGTH * (inverse * inverse * inverse), 0.0)

def operate(field, stiffness):
    padded = jnp.pad(field, ((0, 0), (1, 1), (1, 1), (1, 1)))
    beside = padded[:, 2:, 1:-1, 1:-1] + padded[:, :-2, 1:-1, 1:-1]
    beside = beside + padded[:, 1:-1, 2:, 1:-1] + padded[:, 1:-1, :-2, 1:-1]
    beside = beside + padded[:, 1:-1, 1:-1, 2:] + padded[:, 1:-1, 1:-1, :-2]
    return (6.0 + stiffness) * field - beside

def reference(seg_pos, burgers, seg_tile, quad_pos, quad_node, stiffness):
    group = math.gcd(QPTS, 1024)
    count = QPTS // group
    q_index = jnp.arange(QPTS, dtype=jnp.int32)
    q_tile = q_index // QB
    pos_groups = quad_pos.reshape(3, count, group).transpose(1, 0, 2)
    tile_groups = q_tile.reshape(count, group)

    def traction_group(item):
        weights = near_weights(item[0], item[1], seg_pos, seg_tile)
        return jnp.einsum('gs,cs->cg', weights, burgers, precision=HIGH)
    traction = lax.map(traction_group, (pos_groups, tile_groups))
    traction = traction.transpose(1, 0, 2).reshape(3, QPTS) * (1.0 / math.sqrt(SEGS))
    part = q_index % QB // Q_DEV
    first = quad_node // (NY * CZ)
    second = quad_node // CZ % NY
    third = quad_node % CZ
    flat = ((part * CX + first) * NY + second) * NZ + q_tile * CZ + third
    load = jnp.zeros((3, NX * NY * NZ), dtype=traction.dtype).at[:, flat].add(traction)
    load = load.reshape(3, NX, NY, NZ)
    correction = jnp.zeros_like(load)
    residual, direction = (load, load)
    norm_now = jnp.sum(residual * residual)
    for step in range(ITERS):
        image = operate(direction, stiffness)
        alpha = norm_now / jnp.sum(direction * image)
        correction = correction + alpha * direction
        residual = residual - alpha * image
        norm_next = jnp.sum(residual * residual)
        direction = residual + norm_next / norm_now * direction
        norm_now = norm_next
    motion = correction.reshape(3, NX * NY * NZ)[:, flat]
    motion_groups = motion.reshape(3, count, group).transpose(1, 0, 2)

    def stress_group(total, item):
        weights = near_weights(item[0], item[1], seg_pos, seg_tile)
        return (total + jnp.einsum('gs,cg->cs', weights, item[2], precision=HIGH), None)
    stress, unused = lax.scan(stress_group, jnp.zeros((3, SEGS), dtype=motion.dtype), (pos_groups, tile_groups, motion_groups))
    return (correction, stress * (4.0 / math.sqrt(QPTS)))
```

```python
import math

import jax
import jax.numpy as jnp
from jax import lax
from jax.experimental import pallas as pl
from jax.experimental.pallas import tpu as pltpu
from jax.sharding import PartitionSpec as P

CORE = 0.0001
STRENGTH = 0.001
HIGH = lax.Precision.HIGHEST
F32 = jnp.float32
BF16 = jnp.bfloat16
ROWS = 8
LANES = 128
CHUNK = 256
NT = (((1,), (1,)), ((), ()))
VMEM_LIMIT = 48 * 1024 * 1024


def iota(shape, dim):
    return lax.broadcasted_iota(jnp.int32, shape, dim)


def split(x):
    hi = x.astype(BF16)
    return hi, (x - hi.astype(F32)).astype(BF16)


def near_rank(tile, block):
    near = jnp.abs(tile - block) <= 1
    mask = jnp.where(near, 1.0, 0.0)
    n = tile.shape[1]
    before = jnp.where(iota((n, n), 0) < iota((n, n), 1), 1.0, 0.0)
    rank = jnp.dot(jnp.broadcast_to(mask, (ROWS, n)), before, preferred_element_type=F32)[:1]
    place = jnp.where(iota((n, n), 0) == rank.astype(jnp.int32), mask, 0.0)
    return mask, place


def pack_kernel(where_ref, pos_ref, burgers_ref, tile_ref, out_ref, vals):
    mask, place = near_rank(tile_ref[...], where_ref[1])
    vals[0:3, :] = pos_ref[...]
    vals[3:6, :] = burgers_ref[...]
    vals[6:8, :] = jnp.broadcast_to(mask, (2, mask.shape[1]))
    packed = lax.dot_general(vals[...], place, NT, precision=HIGH, preferred_element_type=F32)
    out_ref[...] = jnp.broadcast_to(packed[None], out_ref.shape)


def assemble(groups_ref, sbuf):
    n_groups, _, width = groups_ref.shape
    offset = jnp.int32(0)
    places = []
    for r in range(n_groups):
        group = groups_ref[r]
        count = jnp.sum(group[6:7, :]).astype(jnp.int32)
        sbuf[pl.ds(pl.multiple_of(offset, ROWS), width), 0:ROWS] = group.T
        places.append((offset, count))
        offset = offset + (count + (ROWS - 1)) // ROWS * ROWS
    sbuf[pl.ds(pl.multiple_of(offset, ROWS), CHUNK), 0:ROWS] = jnp.zeros((CHUNK, ROWS), F32)
    return places, (offset + (CHUNK - 1)) // CHUNK


def spread(sbuf, wide, start):
    for d in range(3):
        wide[d] = jnp.broadcast_to(sbuf[pl.ds(start, CHUNK), d : d + 1], (CHUNK, LANES))


def cubes(wide, q_ref, start, width):
    his, los = [], []
    for j in range(width // LANES):
        at = pl.ds(pl.multiple_of(start + j * LANES, LANES), LANES)
        dx = wide[0] - q_ref[0:1, at]
        dy = wide[1] - q_ref[1:2, at]
        dz = wide[2] - q_ref[2:3, at]
        inverse = lax.rsqrt((dx * dx + CORE) + (dy * dy + dz * dz))
        hi, lo = split(inverse * inverse * inverse)
        his.append(hi)
        los.append(lo)
    return jnp.concatenate(his, axis=1), jnp.concatenate(los, axis=1)


def traction_kernel(scale, groups_ref, q_ref, out_ref, sbuf, wide, total):
    q_dev = q_ref.shape[1]
    _, n_chunks = assemble(groups_ref, sbuf)
    total[...] = jnp.zeros_like(total)

    def chunk(i, carry):
        start = pl.multiple_of(i * CHUNK, CHUNK)
        spread(sbuf, wide, start)
        vectors = jnp.concatenate(split(sbuf[pl.ds(start, CHUNK), 0:ROWS].T), axis=0)
        vectors = jnp.concatenate([vectors, vectors], axis=1)

        def block(j, c):
            at = pl.multiple_of(j * CHUNK, CHUNK)
            hi, lo = cubes(wide, q_ref, at, CHUNK)
            weights = jnp.concatenate([hi, lo], axis=0)
            total[:, pl.ds(at, CHUNK)] += jnp.dot(vectors, weights, preferred_element_type=F32)
            return c

        return lax.fori_loop(0, q_dev // CHUNK, block, carry, unroll=2)

    lax.fori_loop(0, n_chunks, chunk, jnp.int32(0))
    both = (total[0:ROWS, :] + total[ROWS : 2 * ROWS, :]) * scale
    out_ref[...] = jnp.zeros_like(out_ref)
    out_ref[0:3, :] = both[3:6, :]


def row_hot(nodes, k, rows, first):
    row = nodes[k : k + 1, :] // LANES - first
    return jnp.where(iota((rows, LANES), 0) == row, 1.0, 0.0).astype(BF16)


def layers(nodes, t_ref, rows, first, hot, cols):
    n = nodes.shape[0]
    for k in range(n):
        at = slice(k * LANES, (k + 1) * LANES)
        hot[0:rows, at] = row_hot(nodes, k, rows, first)
        here = iota((LANES, LANES), 0) == nodes[k : k + 1, :] % LANES
        for c in range(3):
            value = t_ref[c : c + 1, at]
            hi = value.astype(BF16).astype(F32)
            for p, part in enumerate((hi, value - hi)):
                to = (p * 3 + c) * LANES
                cols[to : to + LANES, at] = jnp.where(here, part, 0.0).astype(BF16)
    out = lax.dot_general(hot[0:rows, :], cols[...], NT, preferred_element_type=F32)
    half = 3 * LANES
    return out[:, :half] + out[:, half:]


def scatter_kernel(where_ref, nodes_ref, t_ref, b_ref, low_ref, high_ref, hot, cols, ends):
    n = t_ref.shape[1] // LANES
    rows = b_ref.shape[1]
    nodes = nodes_ref[pl.ds(pl.multiple_of(where_ref[0] * n, n), n), :]
    load = layers(nodes, t_ref, rows, 0, hot, cols)
    for c in range(3):
        b_ref[c] = load[:, c * LANES : (c + 1) * LANES]
    for k in range(n):
        at = slice(k * LANES, (k + 1) * LANES)
        last = nodes[k : k + 1, :] % LANES
        value = t_ref[:, at]
        hi = value.astype(BF16).astype(F32)
        for p, part in enumerate((hi, value - hi)):
            ends[p * 16 : p * 16 + 8, at] = jnp.where(last == 0, part, 0.0)
            ends[p * 16 + 8 : p * 16 + 16, at] = jnp.where(last == LANES - 1, part, 0.0)
    faces = lax.dot_general(ends[...].astype(BF16), hot[...], NT, preferred_element_type=F32)
    low_ref[...] = faces[0:8] + faces[16:24]
    high_ref[...] = faces[8:16] + faces[24:32]


def beside_in_layer(f):
    i, j = iota(f.shape, 0), iota(f.shape, 1)
    n, m = f.shape
    up = jnp.where(i == 0, 0.0, pltpu.roll(f, 1, 0)) + jnp.where(i == n - 1, 0.0, pltpu.roll(f, n - 1, 0))
    return up + (jnp.where(j == 0, 0.0, pltpu.roll(f, 1, 1)) + jnp.where(j == m - 1, 0.0, pltpu.roll(f, m - 1, 1)))


def operate_kernel(
    n_seg, where_ref, nodes_ref, b_ref, left_ref, right_ref, below_ref, above_ref, k_ref, kr_ref,
    u_ref, g_ref, low_ref, high_ref, corner_ref, sums_ref, hot, cols, parts,
):
    n = left_ref.shape[1] // LANES
    rows = b_ref.shape[1]
    wide = rows // LANES
    me = where_ref[0]

    def nodes_of(r):
        return nodes_ref[pl.ds(pl.multiple_of(r * n, n), n), :]

    left = layers(nodes_of(jnp.maximum(me - 1, 0)), left_ref, LANES, rows - LANES, hot, cols)
    right = layers(nodes_of(jnp.minimum(me + 1, n_seg - 1)), right_ref, 2 * LANES, 0, hot, cols)
    below, above = below_ref[...].T, above_ref[...].T
    lane = iota((LANES, LANES), 1)
    zero = jnp.zeros((LANES, LANES), F32)
    bb, bu, uu, uau = zero, zero, zero, zero
    not_last = jnp.where(me < n_seg - 1, 1.0, 0.0)
    low_ref[...] = jnp.zeros_like(low_ref)
    high_ref[...] = jnp.zeros_like(high_ref)
    corner_ref[...] = jnp.zeros_like(corner_ref)
    for c in range(3):
        comp = slice(c * LANES, (c + 1) * LANES)
        b4, b5 = right[0:LANES, comp], right[LANES : 2 * LANES, comp]
        field = [left[:, comp]] + [b_ref[c, x * LANES : (x + 1) * LANES, :] for x in range(wide)] + [b4]
        us = []
        for x in range(wide):
            at = slice(x * LANES, (x + 1) * LANES)
            f = field[x + 1]
            beside = beside_in_layer(f) + (field[x] + field[x + 2])
            beside = beside + jnp.where(lane == 0, below[at, c : c + 1], 0.0)
            beside = beside + jnp.where(lane == LANES - 1, above[at, c : c + 1], 0.0)
            u = (6.0 + k_ref[at, :]) * f - beside
            u_ref[c, at, :] = u
            us.append(u)
            bb = bb + f * f
            bu = bu + f * u
            uu = uu + u * u
            b_hi, b_lo = split(f.T)
            u_t = u.T
            u_hi, u_lo = split(u_t)
            low_ref[c : c + 1, at] = u_t[0:1, :]
            high_ref[c : c + 1, at] = u_t[LANES - 1 : LANES, :]
            for place, hi, lo in ((c, b_hi, b_lo), (c + 3, u_hi, u_lo)):
                to = slice(place * LANES, (place + 1) * LANES)
                parts[to, at] = hi
                parts[to, rows + x * LANES : rows + (x + 1) * LANES] = lo
        ur = (6.0 + kr_ref[...]) * b4 - (field[wide] + b5 + beside_in_layer(b4))
        for x in range(wide):
            at = slice(x * LANES, (x + 1) * LANES)
            au = (6.0 + k_ref[at, :]) * us[x] - beside_in_layer(us[x])
            if x + 1 < wide:
                au = au - 2.0 * us[x + 1]
            else:
                au = au - (2.0 * not_last) * ur
            uau = uau + us[x] * au
        b4_t = b4.T
        corner_ref[c : c + 1, 0:LANES] = b4_t[0:1, :]
        corner_ref[c : c + 1, LANES : 2 * LANES] = b4_t[LANES - 1 : LANES, :]
    line = iota((1, LANES), 1)
    sums = jnp.zeros((1, LANES), F32)
    for i, part in enumerate((bb, bu, uu, uau)):
        sums = sums + jnp.where(line == i, jnp.sum(part), 0.0)
    sums_ref[...] = jnp.broadcast_to(sums, sums_ref.shape)

    nodes = nodes_of(me)
    g_ref[...] = jnp.zeros_like(g_ref)
    for k in range(0, n, 2):
        here = jnp.concatenate([row_hot(nodes, k, rows, 0), row_hot(nodes, k + 1, rows, 0)], axis=1)
        here = jnp.concatenate([here, here], axis=0)
        found = jnp.dot(parts[...], here, preferred_element_type=F32)
        last = jnp.concatenate([nodes[k : k + 1, :], nodes[k + 1 : k + 2, :]], axis=1) % LANES
        pick = iota((LANES, 2 * LANES), 0) == last
        for v in range(6):
            value = jnp.where(pick, found[v * LANES : (v + 1) * LANES, :], 0.0)
            g_ref[v : v + 1, k * LANES : (k + 2) * LANES] = jnp.sum(value, axis=0, keepdims=True)


def stress_kernel(groups_ref, q_ref, g_ref, out_ref, sbuf, wide, results, motion):
    q_dev = q_ref.shape[1]
    places, n_chunks = assemble(groups_ref, sbuf)
    hi, lo = split(g_ref[...])
    motion[...] = jnp.concatenate([hi, lo], axis=0)

    def chunk(i, carry):
        start = pl.multiple_of(i * CHUNK, CHUNK)
        spread(sbuf, wide, start)

        def block(j, total):
            at = pl.multiple_of(j * CHUNK, CHUNK)
            hi, lo = cubes(wide, q_ref, at, CHUNK)
            weights = jnp.concatenate([hi, lo], axis=1)
            m = motion[:, pl.ds(at, CHUNK)]
            m = jnp.concatenate([m, m], axis=1)
            return total + lax.dot_general(weights, m, NT, preferred_element_type=F32)

        results[pl.ds(start, CHUNK), 0 : 2 * ROWS] = lax.fori_loop(
            0, q_dev // CHUNK, block, jnp.zeros((CHUNK, 2 * ROWS), F32), unroll=2
        )
        return carry

    lax.fori_loop(0, n_chunks, chunk, jnp.int32(0))
    width = groups_ref.shape[2]
    for r, (offset, count) in enumerate(places):
        found = results[pl.ds(pl.multiple_of(offset, ROWS), width), 0 : 2 * ROWS].T
        found = found[0:ROWS] + found[ROWS : 2 * ROWS]
        out_ref[r] = jnp.where(iota((ROWS, width), 1) < count, found, 0.0)


def moments_kernel(sums_ref, high_ref, above_ref, below_ref, corner_ref, partial_ref, out_ref):
    rows = high_ref.shape[1]
    above, below = above_ref[...], below_ref[...]
    crossing = jnp.sum(high_ref[...] * above)
    last = slice(rows - LANES, rows)
    crossing = crossing - jnp.sum(above[:, last] * corner_ref[:, LANES : 2 * LANES])
    crossing = crossing - jnp.sum(below[:, last] * corner_ref[:, 0:LANES])
    lane = iota((ROWS, LANES), 1)
    sums = sums_ref[...] - jnp.where(lane == 3, 2.0 * crossing, 0.0)
    row = iota((ROWS, LANES), 0)
    out_ref[...] = jnp.where((row == 6)[None], sums[None], partial_ref[...])


def unpack_kernel(where_ref, tile_ref, partial_ref, out_ref):
    _, place = near_rank(tile_ref[...], where_ref[1])
    total = jnp.sum(partial_ref[...], axis=0)
    spreaded = jnp.dot(total, place, precision=HIGH, preferred_element_type=F32)
    total = jnp.where(iota(total.shape, 0) == 6, total, spreaded)
    out_ref[...] = jnp.broadcast_to(total[None], out_ref.shape)


def finish_kernel(scale, partial_ref, b_ref, u_ref, correction_ref, stress_ref):
    total = jnp.sum(partial_ref[...], axis=0)
    bb, bu, uu, uau = [total[6:7, i : i + 1] for i in range(4)]
    alpha = bb / bu
    later = bb - 2.0 * alpha * bu + alpha * alpha * uu
    beta = later / bb
    grow = 1.0 + beta
    alpha_next = later / (grow * grow * bu - 2.0 * alpha * grow * uu + alpha * alpha * uau)
    on_b = alpha + alpha_next * grow
    on_u = -alpha_next * alpha
    stress_ref[...] = (on_b * total[0:3] + on_u * total[3:6]) * scale
    for c in range(3):
        correction_ref[c] = on_b * b_ref[c] + on_u * u_ref[c]


def call(kernel, out, scratch=(), smem=0, inputs=0, flops=0, moved=0):
    specs = [pl.BlockSpec(memory_space=pltpu.SMEM)] * smem + [pl.BlockSpec(memory_space=pltpu.VMEM)] * inputs
    shapes = [jax.ShapeDtypeStruct(s, F32) for s in out]
    single = len(shapes) == 1
    vmem = pl.BlockSpec(memory_space=pltpu.VMEM)
    return pl.pallas_call(
        kernel,
        out_shape=shapes[0] if single else tuple(shapes),
        in_specs=specs,
        out_specs=vmem if single else (vmem,) * len(shapes),
        scratch_shapes=list(scratch),
        compiler_params=pltpu.CompilerParams(vmem_limit_bytes=VMEM_LIMIT),
        cost_estimate=pl.CostEstimate(flops=flops, bytes_accessed=moved, transcendentals=0),
    )


def shards(seg_pos, burgers, seg_tile, quad_pos, quad_node, stiffness):
    n_seg, n_fe = lax.axis_size("seg"), lax.axis_size("fe")
    column, block = lax.axis_index("seg"), lax.axis_index("fe")
    s_dev = seg_pos.shape[1]
    q_block = quad_pos.shape[1]
    q_dev = q_block // n_seg
    total_segs = s_dev * n_seg
    total_points = q_block * n_fe
    wide, tall, deep = stiffness.shape
    rows = wide * tall
    where = jnp.stack([column, block]).astype(jnp.int32)
    tile = seg_tile.reshape(1, s_dev)
    nodes = quad_node.reshape(q_block // LANES, LANES)
    points = lax.dynamic_slice_in_dim(quad_pos, column * q_dev, q_dev, 1)
    stiff = stiffness.reshape(rows, deep)

    up_seg = [(i, i + 1) for i in range(n_seg - 1)]
    down_seg = [(i + 1, i) for i in range(n_seg - 1)]
    up_fe = [(i, i + 1) for i in range(n_fe - 1)]
    down_fe = [(i + 1, i) for i in range(n_fe - 1)]

    stiff_right = lax.ppermute(stiff[0:LANES], "seg", down_seg)
    packed = call(
        pack_kernel, [(n_seg, ROWS, s_dev)], [pltpu.VMEM((ROWS, s_dev), F32)], smem=1, inputs=3
    )(where, seg_pos, burgers, tile)
    groups = lax.all_to_all(packed, "seg", 0, 0, tiled=True)

    long = total_segs + 2 * CHUNK
    sbuf = pltpu.VMEM((long, LANES), F32)
    spreaded = pltpu.VMEM((3, CHUNK, LANES), F32)

    def traction(*refs):
        traction_kernel(STRENGTH / math.sqrt(total_segs), *refs)

    t = call(
        traction, [(ROWS, q_dev)], [sbuf, spreaded, pltpu.VMEM((2 * ROWS, q_dev), F32)], inputs=2,
        flops=10**9, moved=10**6,
    )(groups, points)
    from_left = lax.ppermute(t, "seg", up_seg)
    from_right = lax.ppermute(t, "seg", down_seg)
    hot = pltpu.VMEM((rows, q_dev), BF16)
    cols = pltpu.VMEM((6 * LANES, q_dev), BF16)
    b, low, high = call(
        scatter_kernel, [(3, rows, deep), (ROWS, rows), (ROWS, rows)],
        [hot, cols, pltpu.VMEM((4 * ROWS, q_dev), F32)], smem=1, inputs=2, flops=2 * 10**9, moved=10**6,
    )(where, nodes, t)
    below = lax.ppermute(high, "fe", up_fe)
    above = lax.ppermute(low, "fe", down_fe)

    def operate(*refs):
        operate_kernel(n_seg, *refs)

    u, motion, low, high, corner, sums = call(
        operate, [(3, rows, deep), (ROWS, q_dev), (ROWS, rows), (ROWS, rows), (ROWS, 2 * LANES), (ROWS, LANES)],
        [hot, cols, pltpu.VMEM((6 * LANES, 2 * rows), BF16)], smem=1, inputs=8, flops=4 * 10**9, moved=4 * 10**6,
    )(where, nodes, b, from_left, from_right, below, above, stiff, stiff_right)
    u_below = lax.ppermute(high, "fe", up_fe)
    u_above = lax.ppermute(low, "fe", down_fe)
    partial = call(
        stress_kernel, [(n_seg, ROWS, s_dev)],
        [sbuf, spreaded, pltpu.VMEM((long, LANES), F32), pltpu.VMEM((2 * ROWS, q_dev), BF16)],
        inputs=3, flops=10**10, moved=10**6,
    )(groups, points, motion)
    partial = call(moments_kernel, [(n_seg, ROWS, s_dev)], inputs=6)(sums, high, u_above, u_below, corner, partial)
    partial = lax.all_to_all(partial, "seg", 0, 0, tiled=True)
    partial = call(unpack_kernel, [(n_fe, ROWS, s_dev)], smem=1, inputs=2)(where, tile, partial)
    partial = lax.all_to_all(partial, "fe", 0, 0, tiled=True)

    def finish(*refs):
        finish_kernel(4.0 * STRENGTH / math.sqrt(total_points), *refs)

    correction, stress = call(finish, [(3, rows, deep), (3, s_dev)], inputs=3)(partial, b, u)
    return correction.reshape(3, wide, tall, deep), stress


def solution(mesh):
    placed = (
        P(None, "seg"),
        P(None, "seg"),
        P("seg"),
        P(None, "fe"),
        P("fe"),
        P("seg", None, "fe"),
    )
    return jax.shard_map(
        shards,
        mesh=mesh,
        in_specs=placed,
        out_specs=(P(None, "seg", None, "fe"), P(None, "seg")),
        check_vma=False,
    )
```

```python
import math

import jax
import jax.numpy as jnp
from jax import lax
from jax.experimental import pallas as pl
from jax.experimental.pallas import tpu as pltpu
from jax.sharding import PartitionSpec as P

CORE = 0.0001
STRENGTH = 0.001
HIGH = lax.Precision.HIGHEST
F32 = jnp.float32
BF16 = jnp.bfloat16
ROWS = 8
LANES = 128
CHUNK = 256
NT = (((1,), (1,)), ((), ()))
VMEM_LIMIT = 40 * 1024 * 1024


def iota(shape, dim):
    return lax.broadcasted_iota(jnp.int32, shape, dim)


def split(x):
    hi = x.astype(BF16)
    return hi, (x - hi.astype(F32)).astype(BF16)


def near_rank(tile, block):
    near = jnp.abs(tile - block) <= 1
    mask = jnp.where(near, 1.0, 0.0)
    n = tile.shape[1]
    before = jnp.where(iota((n, n), 0) < iota((n, n), 1), 1.0, 0.0)
    rank = jnp.dot(jnp.broadcast_to(mask, (ROWS, n)), before, preferred_element_type=F32)[:1]
    place = jnp.where(iota((n, n), 0) == rank.astype(jnp.int32), mask, 0.0)
    return mask, place


def pack_kernel(where_ref, pos_ref, burgers_ref, tile_ref, out_ref, vals):
    mask, place = near_rank(tile_ref[...], where_ref[1])
    vals[0:3, :] = pos_ref[...]
    vals[3:6, :] = burgers_ref[...]
    vals[6:8, :] = jnp.broadcast_to(mask, (2, mask.shape[1]))
    packed = lax.dot_general(vals[...], place, NT, precision=HIGH, preferred_element_type=F32)
    out_ref[...] = jnp.broadcast_to(packed[None], out_ref.shape)


def assemble(groups_ref, sbuf):
    n_groups, _, width = groups_ref.shape
    offset = 0
    places = []
    for r in range(n_groups):
        group = groups_ref[r]
        count = jnp.sum(group[6:7, :]).astype(jnp.int32)
        sbuf[pl.ds(offset, width), 0:ROWS] = group.T
        places.append((offset, count))
        offset = offset + count
    sbuf[pl.ds(offset, CHUNK), 0:ROWS] = jnp.zeros((CHUNK, ROWS), F32)
    return places, offset


def in_chunks(total, chunk):
    half = CHUNK // 2
    whole = total // CHUNK
    rest = total - whole * CHUNK
    n = whole + jnp.where(rest > half, 1, 0)

    def step(i, carry):
        chunk(pl.multiple_of(i * CHUNK, CHUNK), CHUNK)
        return carry

    lax.fori_loop(0, n, step, jnp.int32(0))

    @pl.when(jnp.logical_and(rest > 0, rest <= half))
    def _():
        chunk(pl.multiple_of(whole * CHUNK, CHUNK), half)


def spread(sbuf, wide, start, size):
    for d in range(3):
        wide[d, 0:size] = jnp.broadcast_to(sbuf[pl.ds(start, size), d : d + 1], (size, LANES))


def cubes(wide, q_ref, start, size):
    his, los = [], []
    for j in range(CHUNK // LANES):
        at = pl.ds(pl.multiple_of(start + j * LANES, LANES), LANES)
        dx = wide[0, 0:size] - q_ref[0:1, at]
        dy = wide[1, 0:size] - q_ref[1:2, at]
        dz = wide[2, 0:size] - q_ref[2:3, at]
        inverse = lax.rsqrt((dx * dx + CORE) + (dy * dy + dz * dz))
        hi, lo = split(inverse * inverse * inverse)
        his.append(hi)
        los.append(lo)
    return jnp.concatenate(his, axis=1), jnp.concatenate(los, axis=1)


def traction_kernel(scale, groups_ref, q_ref, kq_ref, out_ref, sbuf, wide, total):
    q_dev = q_ref.shape[1]
    _, length = assemble(groups_ref, sbuf)
    total[...] = jnp.zeros_like(total)

    def chunk(start, size):
        spread(sbuf, wide, start, size)
        vectors = jnp.concatenate(split(sbuf[pl.ds(start, size), 0:ROWS].T), axis=0)
        vectors = jnp.concatenate([vectors, vectors], axis=1)

        def block(j, c):
            at = pl.multiple_of(j * CHUNK, CHUNK)
            hi, lo = cubes(wide, q_ref, at, size)
            weights = jnp.concatenate([hi, lo], axis=0)
            total[:, pl.ds(at, CHUNK)] += jnp.dot(vectors, weights, preferred_element_type=F32)
            return c

        lax.fori_loop(0, q_dev // CHUNK, block, jnp.int32(0), unroll=8)

    in_chunks(length, chunk)
    both = (total[0:ROWS, :] + total[ROWS : 2 * ROWS, :]) * scale
    out_ref[...] = jnp.zeros_like(out_ref)
    out_ref[0:3, :] = both[3:6, :]
    out_ref[3:4, :] = kq_ref[0:1, :]


def nodes_of(nodes_ref, r, n):
    return nodes_ref[pl.ds(pl.multiple_of(r * n, n), n), :]


def row_hot(nodes, k, rows, first):
    row = nodes[k : k + 1, :] // LANES - first
    return jnp.where(iota((rows, LANES), 0) == row, 1.0, 0.0).astype(BF16)


def spread_points(nodes, values, cols):
    for k in range(nodes.shape[0]):
        at = slice(k * LANES, (k + 1) * LANES)
        here = iota((LANES, LANES), 0) == nodes[k : k + 1, :] % LANES
        for c in range(3):
            value = values[c : c + 1, at]
            hi = value.astype(BF16).astype(F32)
            for p, part in enumerate((hi, value - hi)):
                to = (p * 3 + c) * LANES
                cols[to : to + LANES, at] = jnp.where(here, part, 0.0).astype(BF16)


def layers(hot, cols):
    out = lax.dot_general(hot, cols, NT, preferred_element_type=F32)
    half = 3 * LANES
    return out[:, :half] + out[:, half:]


def set_parts(parts, place, x, rows, tile):
    hi, lo = split(tile)
    to = slice(place * LANES, (place + 1) * LANES)
    parts[to, x * LANES : (x + 1) * LANES] = hi
    parts[to, rows + x * LANES : rows + (x + 1) * LANES] = lo


def pair(nodes, k):
    return jnp.concatenate([nodes[k : k + 1, :], nodes[k + 1 : k + 2, :]], axis=1)


def pair_hot(nodes, k, rows):
    return jnp.concatenate([row_hot(nodes, k, rows, 0), row_hot(nodes, k + 1, rows, 0)], axis=1)


def gather(nodes, parts, rows, fields, out_ref, first):
    for k in range(0, nodes.shape[0], 2):
        here = pair_hot(nodes, k, rows)
        found = jnp.dot(parts[...], jnp.concatenate([here, here], axis=0), preferred_element_type=F32)
        pick = iota((LANES, 2 * LANES), 0) == pair(nodes, k) % LANES
        for f in range(fields):
            value = jnp.where(pick, found[f * LANES : (f + 1) * LANES, :], 0.0)
            out_ref[first + f : first + f + 1, k * LANES : (k + 2) * LANES] = jnp.sum(value, axis=0, keepdims=True)


def stiffness_kernel(where_ref, nodes_ref, k_ref, kq_ref, kz_ref, parts):
    rows = k_ref.shape[0]
    n = kq_ref.shape[1] // LANES
    kz_ref[...] = jnp.zeros_like(kz_ref)
    for x in range(rows // LANES):
        at = slice(x * LANES, (x + 1) * LANES)
        tile = k_ref[at, :].T
        kz_ref[0:1, at] = tile[0:1, :]
        set_parts(parts, 0, x, rows, tile)
    kq_ref[...] = jnp.zeros_like(kq_ref)
    gather(nodes_of(nodes_ref, where_ref[0], n), parts, rows, 1, kq_ref, 0)


def scatter_kernel(where_ref, nodes_ref, t_ref, b_ref, g_ref, low_ref, next_ref, high_ref, hot, cols, parts):
    n = t_ref.shape[1] // LANES
    rows = b_ref.shape[1]
    nodes = nodes_of(nodes_ref, where_ref[0], n)
    for k in range(n):
        hot[:, k * LANES : (k + 1) * LANES] = row_hot(nodes, k, rows, 0)
    spread_points(nodes, t_ref, cols)
    load = layers(hot[...], cols[...])
    for ref in (low_ref, next_ref, high_ref):
        ref[...] = jnp.zeros_like(ref)
    for c in range(3):
        for x in range(rows // LANES):
            at = slice(x * LANES, (x + 1) * LANES)
            f = load[at, c * LANES : (c + 1) * LANES]
            b_ref[c, at, :] = f
            tile = f.T
            set_parts(parts, c, x, rows, tile)
            low_ref[c : c + 1, at] = tile[0:1, :]
            next_ref[c : c + 1, at] = tile[1:2, :]
            high_ref[c : c + 1, at] = tile[LANES - 1 : LANES, :]
    g_ref[...] = jnp.zeros_like(g_ref)
    gather(nodes, parts, rows, 3, g_ref, 0)


def sides_kernel(
    n_seg, where_ref, nodes_ref, left_ref, right_ref, low_ref, next_ref, high_ref, kz_ref,
    sides_ref, down_ref, up_ref, hot, cols,
):
    n = left_ref.shape[1] // LANES
    rows = low_ref.shape[1]
    me = where_ref[0]
    down_ref[...] = jnp.zeros_like(down_ref)
    up_ref[...] = jnp.zeros_like(up_ref)
    own = slice(LANES, LANES + rows)
    down_ref[0:3, own] = low_ref[0:3, :]
    down_ref[3:6, own] = next_ref[0:3, :]
    down_ref[6:7, own] = kz_ref[0:1, :]
    up_ref[0:3, own] = high_ref[0:3, :]

    nodes = nodes_of(nodes_ref, jnp.maximum(me - 1, 0), n)
    for k in range(n):
        hot[0:LANES, k * LANES : (k + 1) * LANES] = row_hot(nodes, k, LANES, rows - LANES)
    spread_points(nodes, left_ref[...] * jnp.where(me > 0, 1.0, 0.0), cols)
    left = layers(hot[0:LANES, :], cols[...])
    nodes = nodes_of(nodes_ref, jnp.minimum(me + 1, n_seg - 1), n)
    for k in range(n):
        hot[:, k * LANES : (k + 1) * LANES] = row_hot(nodes, k, 2 * LANES, 0)
    t = right_ref[...] * jnp.where(me < n_seg - 1, 1.0, 0.0)
    spread_points(nodes, t, cols)
    right = layers(hot[...], cols[...])
    spread_points(nodes, t[0:3] * right_ref[3:4, :], cols)
    stiff = layers(hot[0:LANES, :], cols[...])
    last = slice(LANES + rows, 2 * LANES + rows)
    for c in range(3):
        comp = slice(c * LANES, (c + 1) * LANES)
        sides_ref[c] = left[:, comp]
        sides_ref[3 + c] = right[0:LANES, comp]
        sides_ref[6 + c] = right[LANES : 2 * LANES, comp]
        sides_ref[9 + c] = stiff[:, comp]
        down_ref[c : c + 1, 0:LANES] = left[:, comp].T[0:1, :]
        tile = right[0:LANES, comp].T
        down_ref[c : c + 1, last] = tile[0:1, :]
        up_ref[c : c + 1, last] = tile[LANES - 1 : LANES, :]


def beside_in_layer(f):
    i, j = iota(f.shape, 0), iota(f.shape, 1)
    n, m = f.shape
    up = jnp.where(i == 0, 0.0, pltpu.roll(f, 1, 0)) + jnp.where(i == n - 1, 0.0, pltpu.roll(f, n - 1, 0))
    return up + (jnp.where(j == 0, 0.0, pltpu.roll(f, 1, 1)) + jnp.where(j == m - 1, 0.0, pltpu.roll(f, m - 1, 1)))


def operate_kernel(where_ref, nodes_ref, b_ref, sides_ref, k_ref, g_ref, u_ref, ur_ref, motion_ref, high_ref, parts):
    n = g_ref.shape[1] // LANES
    rows = b_ref.shape[1]
    wide = rows // LANES
    high_ref[...] = jnp.zeros_like(high_ref)
    for c in range(3):
        b4 = sides_ref[3 + c]
        field = [sides_ref[c]] + [b_ref[c, x * LANES : (x + 1) * LANES, :] for x in range(wide)] + [b4]
        for x in range(wide):
            at = slice(x * LANES, (x + 1) * LANES)
            f = field[x + 1]
            u = (6.0 + k_ref[at, :]) * f - (beside_in_layer(f) + (field[x] + field[x + 2]))
            u_ref[c, at, :] = u
            tile = u.T
            high_ref[c : c + 1, at] = tile[LANES - 1 : LANES, :]
            set_parts(parts, c, x, rows, tile)
        ur_ref[c] = 6.0 * b4 + sides_ref[9 + c] - (field[wide] + sides_ref[6 + c] + beside_in_layer(b4))
    motion_ref[...] = g_ref[...]
    gather(nodes_of(nodes_ref, where_ref[0], n), parts, rows, 3, motion_ref, 3)


def ends_kernel(
    n_seg, n_fe, where_ref, nodes_ref, b_ref, u_ref, ur_ref, k_ref, above_ref, below_ref, uh_ref, high_ref, g_ref,
    out_ref, motion_ref, sums_ref,
):
    n = g_ref.shape[1] // LANES
    rows = b_ref.shape[1]
    wide = rows // LANES
    me, block = where_ref[0], where_ref[1]
    is_above = jnp.where(block < n_fe - 1, 1.0, 0.0)
    above = above_ref[...] * is_above
    below = below_ref[...] * jnp.where(block > 0, 1.0, 0.0)
    own = slice(LANES, LANES + rows)

    center = above[0:3, own]
    place = iota(center.shape, 1) % LANES
    beside = above[0:3, 0:rows] + above[0:3, 2 * LANES : 2 * LANES + rows]
    beside = beside + jnp.where(place == 0, 0.0, pltpu.roll(center, 1, 1))
    beside = beside + jnp.where(place == LANES - 1, 0.0, pltpu.roll(center, rows - 1, 1))
    beside = beside + high_ref[0:3, :] + above[3:6, own]
    next_u = (6.0 + above[6:7, own]) * center - beside
    crossing = is_above * jnp.sum((uh_ref[0:3, :] - center) * next_u)

    above_t, below_t = above.T, below.T
    lane = iota((LANES, LANES), 1)
    zero = jnp.zeros((LANES, LANES), F32)
    bb, bu, uu, uau = zero, zero, zero, zero
    not_last = jnp.where(me < n_seg - 1, 2.0, 0.0)

    def ends(c, x):
        at = slice((x + 1) * LANES, (x + 2) * LANES)
        low = jnp.where(lane == 0, below_t[at, c : c + 1], 0.0)
        return low + jnp.where(lane == LANES - 1, above_t[at, c : c + 1], 0.0)

    for c in range(3):
        us = []
        for x in range(wide):
            at = slice(x * LANES, (x + 1) * LANES)
            f = b_ref[c, at, :]
            u = u_ref[c, at, :] - ends(c, x)
            out_ref[c, at, :] = u
            us.append(u)
            bb = bb + f * f
            bu = bu + f * u
            uu = uu + u * u
        us.append(not_last * (ur_ref[c] - ends(c, wide)))
        for x in range(wide):
            at = slice(x * LANES, (x + 1) * LANES)
            beside = beside_in_layer(us[x]) + (us[x + 1] if x + 1 == wide else 2.0 * us[x + 1])
            uau = uau + us[x] * ((6.0 + k_ref[at, :]) * us[x] - beside)
    line = iota((1, LANES), 1)
    sums = jnp.where(line == 3, -2.0 * crossing, 0.0)
    for i, part in enumerate((bb, bu, uu, uau)):
        sums = sums + jnp.where(line == i, jnp.sum(part), 0.0)
    sums_ref[...] = jnp.broadcast_to(sums, sums_ref.shape)

    nodes = nodes_of(nodes_ref, me, n)
    faces = jnp.concatenate(split(below[:, own]) + split(above[:, own]), axis=0)
    motion_ref[...] = g_ref[...]
    for k in range(0, n, 2):
        at = slice(k * LANES, (k + 2) * LANES)
        found = jnp.dot(faces, pair_hot(nodes, k, rows), preferred_element_type=F32)
        last = pair(nodes, k) % LANES
        extra = jnp.where(last == 0, found[0:3] + found[8:11], 0.0)
        extra = extra + jnp.where(last == LANES - 1, found[16:19] + found[24:27], 0.0)
        motion_ref[3:6, at] = g_ref[3:6, at] - extra


def stress_kernel(groups_ref, q_ref, g_ref, sums_ref, out_ref, sbuf, wide, results, motion):
    q_dev = q_ref.shape[1]
    places, length = assemble(groups_ref, sbuf)
    motion[...] = jnp.concatenate(split(g_ref[...]), axis=0)

    def chunk(start, size):
        spread(sbuf, wide, start, size)

        def block(j, total):
            at = pl.multiple_of(j * CHUNK, CHUNK)
            weights = jnp.concatenate(cubes(wide, q_ref, at, size), axis=1)
            m = motion[:, pl.ds(at, CHUNK)]
            m = jnp.concatenate([m, m], axis=1)
            return total + lax.dot_general(weights, m, NT, preferred_element_type=F32)

        results[pl.ds(start, size), 0 : 2 * ROWS] = lax.fori_loop(
            0, q_dev // CHUNK, block, jnp.zeros((size, 2 * ROWS), F32), unroll=8
        )

    in_chunks(length, chunk)
    width = groups_ref.shape[2]
    row = iota((ROWS, width), 0)
    for r, (offset, count) in enumerate(places):
        found = results[pl.ds(offset, width), 0 : 2 * ROWS].T
        found = found[0:ROWS] + found[ROWS : 2 * ROWS]
        found = jnp.where(iota((ROWS, width), 1) < count, found, 0.0)
        out_ref[r] = jnp.where(row == 6, sums_ref[...], found)


def unpack_kernel(where_ref, tile_ref, partial_ref, out_ref):
    _, place = near_rank(tile_ref[...], where_ref[1])
    total = jnp.sum(partial_ref[...], axis=0)
    spreaded = jnp.dot(total, place, precision=HIGH, preferred_element_type=F32)
    total = jnp.where(iota(total.shape, 0) == 6, total, spreaded)
    out_ref[...] = jnp.broadcast_to(total[None], out_ref.shape)


def finish_kernel(scale, partial_ref, b_ref, u_ref, correction_ref, stress_ref):
    total = jnp.sum(partial_ref[...], axis=0)
    bb, bu, uu, uau = [total[6:7, i : i + 1] for i in range(4)]
    alpha = bb / bu
    later = bb - 2.0 * alpha * bu + alpha * alpha * uu
    beta = later / bb
    grow = 1.0 + beta
    alpha_next = later / (grow * grow * bu - 2.0 * alpha * grow * uu + alpha * alpha * uau)
    on_b = alpha + alpha_next * grow
    on_u = -alpha_next * alpha
    stress_ref[...] = (on_b * total[0:3] + on_u * total[3:6]) * scale
    for c in range(3):
        correction_ref[c] = on_b * b_ref[c] + on_u * u_ref[c]


def call(kernel, out, scratch=(), smem=0, inputs=0, flops=0, moved=0):
    specs = [pl.BlockSpec(memory_space=pltpu.SMEM)] * smem + [pl.BlockSpec(memory_space=pltpu.VMEM)] * inputs
    shapes = [jax.ShapeDtypeStruct(s, F32) for s in out]
    single = len(shapes) == 1
    vmem = pl.BlockSpec(memory_space=pltpu.VMEM)
    return pl.pallas_call(
        kernel,
        out_shape=shapes[0] if single else tuple(shapes),
        in_specs=specs,
        out_specs=vmem if single else (vmem,) * len(shapes),
        scratch_shapes=list(scratch),
        compiler_params=pltpu.CompilerParams(vmem_limit_bytes=VMEM_LIMIT),
        cost_estimate=pl.CostEstimate(flops=flops, bytes_accessed=moved, transcendentals=0),
    )


def shards(seg_pos, burgers, seg_tile, quad_pos, quad_node, stiffness):
    n_seg, n_fe = lax.axis_size("seg"), lax.axis_size("fe")
    column, block = lax.axis_index("seg"), lax.axis_index("fe")
    s_dev = seg_pos.shape[1]
    q_block = quad_pos.shape[1]
    q_dev = q_block // n_seg
    total_segs = s_dev * n_seg
    total_points = q_block * n_fe
    wide, tall, deep = stiffness.shape
    rows = wide * tall
    where = jnp.stack([column, block]).astype(jnp.int32)
    tile = seg_tile.reshape(1, s_dev)
    nodes = quad_node.reshape(q_block // LANES, LANES)
    points = lax.dynamic_slice_in_dim(quad_pos, column * q_dev, q_dev, 1)
    stiff = stiffness.reshape(rows, deep)

    up_seg = [(i, (i + 1) % n_seg) for i in range(n_seg)]
    down_seg = [((i + 1) % n_seg, i) for i in range(n_seg)]
    up_fe = [(i, (i + 1) % n_fe) for i in range(n_fe)]
    down_fe = [((i + 1) % n_fe, i) for i in range(n_fe)]
    field, line = (3, rows, deep), (ROWS, q_dev)
    face, message = (ROWS, rows), (ROWS, rows + 2 * LANES)
    long = total_segs + 2 * CHUNK
    sbuf = pltpu.VMEM((long, LANES), F32)
    spreaded = pltpu.VMEM((3, CHUNK, LANES), F32)
    cols = pltpu.VMEM((6 * LANES, q_dev), BF16)

    packed = call(
        pack_kernel, [(n_seg, ROWS, s_dev)], [pltpu.VMEM((ROWS, s_dev), F32)], smem=1, inputs=3
    )(where, seg_pos, burgers, tile)
    groups = lax.all_to_all(packed, "seg", 0, 0, tiled=True)
    kq, kz = call(
        stiffness_kernel, [line, face], [pltpu.VMEM((LANES, 2 * rows), BF16)], smem=1, inputs=2,
        flops=10**9, moved=10**6,
    )(where, nodes, stiff)

    def traction(*refs):
        traction_kernel(STRENGTH / math.sqrt(total_segs), *refs)

    t = call(
        traction, [line], [sbuf, spreaded, pltpu.VMEM((2 * ROWS, q_dev), F32)], inputs=3,
        flops=10**10, moved=10**6,
    )(groups, points, kq)
    from_left = lax.ppermute(t, "seg", up_seg)
    from_right = lax.ppermute(t, "seg", down_seg)
    b, g, low, after, high = call(
        scatter_kernel, [field, line, face, face, face],
        [pltpu.VMEM((rows, q_dev), BF16), cols, pltpu.VMEM((3 * LANES, 2 * rows), BF16)],
        smem=1, inputs=2, flops=4 * 10**9, moved=4 * 10**6,
    )(where, nodes, t)

    def fill_sides(*refs):
        sides_kernel(n_seg, *refs)

    sides, down, up = call(
        fill_sides, [(12, tall, deep), message, message], [pltpu.VMEM((2 * LANES, q_dev), BF16), cols],
        smem=1, inputs=7, flops=2 * 10**9, moved=10**6,
    )(where, nodes, from_left, from_right, low, after, high, kz)
    above = lax.ppermute(down, "fe", down_fe)
    below = lax.ppermute(up, "fe", up_fe)
    u, ur, g, uh = call(
        operate_kernel, [field, (3, tall, deep), line, face], [pltpu.VMEM((3 * LANES, 2 * rows), BF16)],
        smem=1, inputs=5, flops=4 * 10**9, moved=4 * 10**6,
    )(where, nodes, b, sides, stiff, g)

    def fill_ends(*refs):
        ends_kernel(n_seg, n_fe, *refs)

    u, motion, sums = call(
        fill_ends, [field, line, (ROWS, LANES)], smem=1, inputs=10, flops=10**9, moved=4 * 10**6
    )(where, nodes, b, u, ur, stiff, above, below, uh, high, g)
    partial = call(
        stress_kernel, [(n_seg, ROWS, s_dev)],
        [sbuf, spreaded, pltpu.VMEM((long, LANES), F32), pltpu.VMEM((2 * ROWS, q_dev), BF16)],
        inputs=4, flops=10**10, moved=10**6,
    )(groups, points, motion, sums)
    partial = lax.all_to_all(partial, "seg", 0, 0, tiled=True)
    partial = call(unpack_kernel, [(n_fe, ROWS, s_dev)], smem=1, inputs=2)(where, tile, partial)
    partial = lax.all_to_all(partial, "fe", 0, 0, tiled=True)

    def finish(*refs):
        finish_kernel(4.0 * STRENGTH / math.sqrt(total_points), *refs)

    correction, stress = call(finish, [(3, rows, deep), (3, s_dev)], inputs=3)(partial, b, u)
    return correction.reshape(3, wide, tall, deep), stress


def solution(mesh):
    placed = (
        P(None, "seg"),
        P(None, "seg"),
        P("seg"),
        P(None, "fe"),
        P("fe"),
        P("seg", None, "fe"),
    )
    return jax.shard_map(
        shards,
        mesh=mesh,
        in_specs=placed,
        out_specs=(P(None, "seg", None, "fe"), P(None, "seg")),
        check_vma=False,
    )
```

```python
import math

import jax
import jax.numpy as jnp
from jax import lax
from jax.experimental import pallas as pl
from jax.experimental.pallas import tpu as pltpu
from jax.sharding import PartitionSpec as P

CORE = 0.0001
STRENGTH = 0.001
HIGH = lax.Precision.HIGHEST
F32 = jnp.float32
BF16 = jnp.bfloat16
ROWS = 8
LANES = 128
CHUNK = 256
KEPT = 7
NT = (((1,), (1,)), ((), ()))
VMEM_LIMIT = 12 * 1024 * 1024


def iota(shape, dim):
    return lax.broadcasted_iota(jnp.int32, shape, dim)


def split(x):
    hi = x.astype(BF16)
    return hi, (x - hi.astype(F32)).astype(BF16)


def near_rank(tile, block):
    near = jnp.abs(tile.astype(jnp.int32) - block) <= 1
    mask = jnp.where(near, 1.0, 0.0)
    n = tile.shape[1]
    before = jnp.where(iota((n, n), 0) < iota((n, n), 1), 1.0, 0.0)
    rank = jnp.dot(jnp.broadcast_to(mask, (ROWS, n)), before, preferred_element_type=F32)[:1]
    place = jnp.where(iota((n, n), 0) == rank.astype(jnp.int32), mask, 0.0)
    return mask, place


def pack_kernel(where_ref, segs_ref, out_ref):
    segs = segs_ref[...]
    mask, place = near_rank(segs[6:7], where_ref[1])
    vals = jnp.where(iota(segs.shape, 0) < 6, segs, mask)
    packed = lax.dot_general(vals, place, NT, precision=HIGH, preferred_element_type=F32)
    out_ref[...] = jnp.broadcast_to(packed[None], out_ref.shape)


def measured(groups_ref):
    offset, longest = 0, 0
    places = []
    for r in range(groups_ref.shape[0]):
        count = jnp.sum(groups_ref[r, 6:7, :]).astype(jnp.int32)
        places.append((offset, count))
        offset = offset + count
        longest = jnp.maximum(longest, count)
    return places, offset, longest


def by_width(longest, width, run):
    half = width // 2

    @pl.when(longest <= half)
    def _():
        run(half)

    @pl.when(longest > half)
    def _():
        run(width)


def assemble(groups_ref, sbuf):
    places, total, longest = measured(groups_ref)

    def run(rows):
        for r, (offset, _) in enumerate(places):
            sbuf[pl.ds(offset, rows), 0:ROWS] = groups_ref[r].T[0:rows]

    by_width(longest, groups_ref.shape[2], run)
    sbuf[pl.ds(total, CHUNK), 0:ROWS] = jnp.zeros((CHUNK, ROWS), F32)
    return places, total, longest


def in_chunks(total, chunk):
    half = CHUNK // 2
    whole = total // CHUNK
    rest = total - whole * CHUNK
    n = whole + jnp.where(rest > half, 1, 0)

    def step(i, carry):
        chunk(pl.multiple_of(i * CHUNK, CHUNK), CHUNK)
        return carry

    lax.fori_loop(0, n, step, jnp.int32(0))

    @pl.when(jnp.logical_and(rest > 0, rest <= half))
    def _():
        chunk(pl.multiple_of(whole * CHUNK, CHUNK), half)


def spread(sbuf, wide, start, size):
    for d in range(3):
        wide[d, 0:size] = jnp.broadcast_to(sbuf[pl.ds(start, size), d : d + 1], (size, LANES))


def cubes(wide, q_ref, start, size):
    his, los = [], []
    for j in range(CHUNK // LANES):
        at = pl.ds(pl.multiple_of(start + j * LANES, LANES), LANES)
        dx = wide[0, 0:size] - q_ref[0:1, at]
        dy = wide[1, 0:size] - q_ref[1:2, at]
        dz = wide[2, 0:size] - q_ref[2:3, at]
        inverse = lax.rsqrt((dx * dx + CORE) + (dy * dy + dz * dz))
        hi, lo = split(inverse * inverse * inverse)
        his.append(hi)
        los.append(lo)
    return jnp.concatenate(his, axis=1), jnp.concatenate(los, axis=1)


def traction_kernel(scale, groups_ref, q_ref, kq_ref, out_ref, sent_ref, kept_ref, sbuf, wide, total):
    q_dev = q_ref.shape[1]
    _, length, _ = assemble(groups_ref, sbuf)
    total[...] = jnp.zeros_like(total)

    def chunk(start, size):
        spread(sbuf, wide, start, size)
        vectors = jnp.concatenate(split(sbuf[pl.ds(start, size), 0:ROWS].T), axis=0)
        vectors = jnp.concatenate([vectors, vectors], axis=1)
        slot = jnp.minimum(start // CHUNK, KEPT)

        def block(j, c):
            at = pl.multiple_of(j * CHUNK, CHUNK)
            hi, lo = cubes(wide, q_ref, at, size)
            kept_ref[slot, 0, 0:size, pl.ds(at, CHUNK)] = hi
            kept_ref[slot, 1, 0:size, pl.ds(at, CHUNK)] = lo
            weights = jnp.concatenate([hi, lo], axis=0)
            total[:, pl.ds(at, CHUNK)] += jnp.dot(vectors, weights, preferred_element_type=F32)
            return c

        lax.fori_loop(0, q_dev // CHUNK, block, jnp.int32(0), unroll=8)

    in_chunks(length, chunk)
    both = (total[0:ROWS, :] + total[ROWS : 2 * ROWS, :]) * scale
    out_ref[...] = jnp.zeros_like(out_ref)
    out_ref[0:3, :] = both[3:6, :]
    half = q_dev // 2
    for p in range(2):
        at = slice(p * half, (p + 1) * half)
        sent_ref[4 * p : 4 * p + 3, :] = both[3:6, at]
        sent_ref[4 * p + 3 : 4 * p + 4, :] = kq_ref[0:1, at]


def nodes_of(nodes_ref, r, n):
    return nodes_ref[pl.ds(pl.multiple_of(r * n, n), n), :]


def set_hot(nodes, out_ref, first):
    rows = out_ref.shape[0]
    for k in range(nodes.shape[0]):
        row = nodes[k : k + 1, :] // LANES - first
        here = jnp.where(iota((rows, LANES), 0) == row, 1.0, 0.0)
        out_ref[:, k * LANES : (k + 1) * LANES] = here.astype(BF16)


def set_spot(nodes, out_ref):
    for k in range(nodes.shape[0]):
        here = jnp.where(iota((LANES, LANES), 0) == nodes[k : k + 1, :] % LANES, 1.0, 0.0)
        out_ref[:, k * LANES : (k + 1) * LANES] = here.astype(BF16)


def spread_points(spot_ref, values, cols):
    n = spot_ref.shape[1]
    for p, parts in enumerate(split(values)):
        for c in range(3):
            to = (p * 3 + c) * LANES
            for k in range(0, n, CHUNK):
                at = slice(k, k + CHUNK)
                part = jnp.broadcast_to(parts[c : c + 1, at], (LANES, CHUNK))
                cols[to : to + LANES, at] = spot_ref[:, at] * part


def layers(hot, cols):
    out = lax.dot_general(hot, cols, NT, preferred_element_type=F32)
    half = 3 * LANES
    return out[:, :half] + out[:, half:]


def set_parts(parts, place, x, rows, tile):
    hi, lo = split(tile)
    to = slice(place * LANES, (place + 1) * LANES)
    parts[to, x * LANES : (x + 1) * LANES] = hi
    parts[to, rows + x * LANES : rows + (x + 1) * LANES] = lo


def pair(nodes, k):
    return jnp.concatenate([nodes[k : k + 1, :], nodes[k + 1 : k + 2, :]], axis=1)


def gather(nodes, hot_ref, parts, fields, out_ref, first):
    for k in range(0, nodes.shape[0], 2):
        at = slice(k * LANES, (k + 2) * LANES)
        here = hot_ref[0 : parts.shape[1] // 2, at]
        found = jnp.dot(parts[...], jnp.concatenate([here, here], axis=0), preferred_element_type=F32)
        pick = iota((LANES, 2 * LANES), 0) == pair(nodes, k) % LANES
        for f in range(fields):
            value = jnp.where(pick, found[f * LANES : (f + 1) * LANES, :], 0.0)
            out_ref[first + f : first + f + 1, at] = jnp.sum(value, axis=0, keepdims=True)


def prepare_kernel(where_ref, nodes_ref, k_ref, kq_ref, kz_ref, hot_ref, parts):
    rows = k_ref.shape[0]
    n = kq_ref.shape[1] // LANES
    nodes = nodes_of(nodes_ref, where_ref[0], n)
    set_hot(nodes, hot_ref.at[0:rows], 0)
    set_spot(nodes, hot_ref.at[rows : rows + LANES])
    kz_ref[...] = jnp.zeros_like(kz_ref)
    for x in range(rows // LANES):
        at = slice(x * LANES, (x + 1) * LANES)
        tile = k_ref[at, :].T
        kz_ref[0:1, at] = tile[0:1, :]
        set_parts(parts, 0, x, rows, tile)
    kq_ref[...] = jnp.zeros_like(kq_ref)
    gather(nodes, hot_ref, parts, 1, kq_ref, 0)


def scatter_kernel(
    n_seg, where_ref, nodes_ref, t_ref, hot_ref, b_ref, g_ref, low_ref, next_ref, high_ref, side_hot_ref, cols, parts
):
    n = t_ref.shape[1] // LANES
    rows = b_ref.shape[1]
    spread_points(hot_ref.at[rows : rows + LANES], t_ref[...], cols)
    load = layers(hot_ref[0:rows, :], cols[...])
    for ref in (low_ref, next_ref, high_ref):
        ref[...] = jnp.zeros_like(ref)
    for c in range(3):
        for x in range(rows // LANES):
            at = slice(x * LANES, (x + 1) * LANES)
            f = load[at, c * LANES : (c + 1) * LANES]
            b_ref[c, at, :] = f
            tile = f.T
            set_parts(parts, c, x, rows, tile)
            low_ref[c : c + 1, at] = tile[0:1, :]
            next_ref[c : c + 1, at] = tile[1:2, :]
            high_ref[c : c + 1, at] = tile[LANES - 1 : LANES, :]
    g_ref[...] = jnp.zeros_like(g_ref)
    me = where_ref[0]
    gather(nodes_of(nodes_ref, me, n), hot_ref, parts, 3, g_ref, 0)
    nodes = nodes_of(nodes_ref, jnp.maximum(me - 1, 0), n)
    set_hot(nodes, side_hot_ref.at[0:LANES], rows - LANES)
    set_spot(nodes, side_hot_ref.at[LANES : 2 * LANES])
    nodes = nodes_of(nodes_ref, jnp.minimum(me + 1, n_seg - 1), n)
    set_hot(nodes, side_hot_ref.at[2 * LANES : 4 * LANES], 0)
    set_spot(nodes, side_hot_ref.at[4 * LANES : 5 * LANES])


def unfold(sent):
    return jnp.concatenate([sent[0:4], sent[4:8]], axis=1)


def sides_kernel(
    n_seg, where_ref, left_ref, right_ref, side_hot_ref, low_ref, next_ref, high_ref, kz_ref,
    sides_ref, down_ref, up_ref, cols,
):
    rows = low_ref.shape[1]
    me = where_ref[0]
    down_ref[...] = jnp.zeros_like(down_ref)
    up_ref[...] = jnp.zeros_like(up_ref)
    own = slice(LANES, LANES + rows)
    down_ref[0:3, own] = low_ref[0:3, :]
    down_ref[3:6, own] = next_ref[0:3, :]
    down_ref[6:7, own] = kz_ref[0:1, :]
    up_ref[0:3, own] = high_ref[0:3, :]

    spread_points(side_hot_ref.at[LANES : 2 * LANES], unfold(left_ref[...]) * jnp.where(me > 0, 1.0, 0.0), cols)
    left = layers(side_hot_ref[0:LANES, :], cols[...])
    t = unfold(right_ref[...])
    kq = t[3:4]
    t = t * jnp.where(me < n_seg - 1, 1.0, 0.0)
    right_spot = side_hot_ref.at[4 * LANES : 5 * LANES]
    spread_points(right_spot, t, cols)
    right = layers(side_hot_ref[2 * LANES : 4 * LANES, :], cols[...])
    spread_points(right_spot, t * kq, cols)
    stiff = layers(side_hot_ref[2 * LANES : 3 * LANES, :], cols[...])
    last = slice(LANES + rows, 2 * LANES + rows)
    for c in range(3):
        comp = slice(c * LANES, (c + 1) * LANES)
        sides_ref[c] = left[:, comp]
        sides_ref[3 + c] = right[0:LANES, comp]
        sides_ref[6 + c] = right[LANES : 2 * LANES, comp]
        sides_ref[9 + c] = stiff[:, comp]
        down_ref[c : c + 1, 0:LANES] = left[:, comp].T[0:1, :]
        tile = right[0:LANES, comp].T
        down_ref[c : c + 1, last] = tile[0:1, :]
        up_ref[c : c + 1, last] = tile[LANES - 1 : LANES, :]


def beside_in_layer(f):
    i, j = iota(f.shape, 0), iota(f.shape, 1)
    n, m = f.shape
    up = jnp.where(i == 0, 0.0, pltpu.roll(f, 1, 0)) + jnp.where(i == n - 1, 0.0, pltpu.roll(f, n - 1, 0))
    return up + (jnp.where(j == 0, 0.0, pltpu.roll(f, 1, 1)) + jnp.where(j == m - 1, 0.0, pltpu.roll(f, m - 1, 1)))


def operate_kernel(
    where_ref, nodes_ref, b_ref, sides_ref, k_ref, g_ref, hot_ref, u_ref, ur_ref, motion_ref, high_ref, parts
):
    n = g_ref.shape[1] // LANES
    rows = b_ref.shape[1]
    wide = rows // LANES
    high_ref[...] = jnp.zeros_like(high_ref)
    for c in range(3):
        b4 = sides_ref[3 + c]
        field = [sides_ref[c]] + [b_ref[c, x * LANES : (x + 1) * LANES, :] for x in range(wide)] + [b4]
        for x in range(wide):
            at = slice(x * LANES, (x + 1) * LANES)
            f = field[x + 1]
            u = (6.0 + k_ref[at, :]) * f - (beside_in_layer(f) + (field[x] + field[x + 2]))
            u_ref[c, at, :] = u
            tile = u.T
            high_ref[c : c + 1, at] = tile[LANES - 1 : LANES, :]
            set_parts(parts, c, x, rows, tile)
        ur_ref[c] = 6.0 * b4 + sides_ref[9 + c] - (field[wide] + sides_ref[6 + c] + beside_in_layer(b4))
    motion_ref[...] = g_ref[...]
    gather(nodes_of(nodes_ref, where_ref[0], n), hot_ref, parts, 3, motion_ref, 3)


def ends_kernel(
    n_seg, n_fe, where_ref, nodes_ref, b_ref, u_ref, ur_ref, k_ref, above_ref, below_ref, uh_ref, high_ref, g_ref,
    hot_ref, out_ref, motion_ref, sums_ref,
):
    n = g_ref.shape[1] // LANES
    rows = b_ref.shape[1]
    wide = rows // LANES
    me, block = where_ref[0], where_ref[1]
    is_above = jnp.where(block < n_fe - 1, 1.0, 0.0)
    above = above_ref[...] * is_above
    below = below_ref[...] * jnp.where(block > 0, 1.0, 0.0)
    own = slice(LANES, LANES + rows)

    center = above[0:3, own]
    place = iota(center.shape, 1) % LANES
    beside = above[0:3, 0:rows] + above[0:3, 2 * LANES : 2 * LANES + rows]
    beside = beside + jnp.where(place == 0, 0.0, pltpu.roll(center, 1, 1))
    beside = beside + jnp.where(place == LANES - 1, 0.0, pltpu.roll(center, rows - 1, 1))
    beside = beside + high_ref[0:3, :] + above[3:6, own]
    next_u = (6.0 + above[6:7, own]) * center - beside
    crossing = is_above * jnp.sum((uh_ref[0:3, :] - center) * next_u)

    above_t, below_t = above.T, below.T
    lane = iota((LANES, LANES), 1)
    zero = jnp.zeros((LANES, LANES), F32)
    bb, bu, uu, uau = zero, zero, zero, zero
    not_last = jnp.where(me < n_seg - 1, 2.0, 0.0)

    def ends(c, x):
        at = slice((x + 1) * LANES, (x + 2) * LANES)
        low = jnp.where(lane == 0, below_t[at, c : c + 1], 0.0)
        return low + jnp.where(lane == LANES - 1, above_t[at, c : c + 1], 0.0)

    for c in range(3):
        us = []
        for x in range(wide):
            at = slice(x * LANES, (x + 1) * LANES)
            f = b_ref[c, at, :]
            u = u_ref[c, at, :] - ends(c, x)
            out_ref[c, at, :] = u
            us.append(u)
            bb = bb + f * f
            bu = bu + f * u
            uu = uu + u * u
        us.append(not_last * (ur_ref[c] - ends(c, wide)))
        for x in range(wide):
            at = slice(x * LANES, (x + 1) * LANES)
            beside = beside_in_layer(us[x]) + (us[x + 1] if x + 1 == wide else 2.0 * us[x + 1])
            uau = uau + us[x] * ((6.0 + k_ref[at, :]) * us[x] - beside)
    line = iota((1, LANES), 1)
    sums = jnp.where(line == 3, -2.0 * crossing, 0.0)
    for i, part in enumerate((bb, bu, uu, uau)):
        sums = sums + jnp.where(line == i, jnp.sum(part), 0.0)
    sums_ref[...] = jnp.broadcast_to(sums, sums_ref.shape)

    nodes = nodes_of(nodes_ref, me, n)
    faces = jnp.concatenate(split(below[:, own]) + split(above[:, own]), axis=0)
    motion_ref[...] = g_ref[...]
    for k in range(0, n, 2):
        at = slice(k * LANES, (k + 2) * LANES)
        found = jnp.dot(faces, hot_ref[0:rows, at], preferred_element_type=F32)
        last = pair(nodes, k) % LANES
        extra = jnp.where(last == 0, found[0:3] + found[8:11], 0.0)
        extra = extra + jnp.where(last == LANES - 1, found[16:19] + found[24:27], 0.0)
        motion_ref[3:6, at] = g_ref[3:6, at] - extra


def stress_kernel(groups_ref, kept_ref, q_ref, g_ref, sums_ref, out_ref, sbuf, wide, results, motion):
    q_dev = q_ref.shape[1]
    n_groups, _, width = out_ref.shape
    places, length, longest = measured(groups_ref)
    motion[...] = jnp.concatenate(split(g_ref[...]), axis=0)
    n_chunks = (length + (CHUNK - 1)) // CHUNK
    n_kept = jnp.minimum(n_chunks, KEPT)

    def from_kept(i, carry):
        m = motion[...]
        found = lax.dot_general(kept_ref[i, 0], m, NT, preferred_element_type=F32)
        found = found + lax.dot_general(kept_ref[i, 1], m, NT, preferred_element_type=F32)
        results[pl.ds(pl.multiple_of(i * CHUNK, CHUNK), CHUNK), 0 : 2 * ROWS] = found
        return carry

    lax.fori_loop(0, n_kept, from_kept, jnp.int32(0))

    def again(i, carry):
        start = pl.multiple_of(i * CHUNK, CHUNK)
        spread(sbuf, wide, start, CHUNK)

        def block(j, total):
            at = pl.multiple_of(j * CHUNK, CHUNK)
            hi, lo = cubes(wide, q_ref, at, CHUNK)
            m = motion[:, pl.ds(at, CHUNK)]
            total = total + lax.dot_general(hi, m, NT, preferred_element_type=F32)
            return total + lax.dot_general(lo, m, NT, preferred_element_type=F32)

        results[pl.ds(start, CHUNK), 0 : 2 * ROWS] = lax.fori_loop(
            0, q_dev // CHUNK, block, jnp.zeros((CHUNK, 2 * ROWS), F32), unroll=8
        )
        return carry

    @pl.when(n_chunks > KEPT)
    def _():
        assemble(groups_ref, sbuf)
        lax.fori_loop(KEPT, n_chunks, again, jnp.int32(0))

    def run(rows):
        row = iota((ROWS, rows), 0)
        for r, (offset, count) in enumerate(places):
            found = results[pl.ds(offset, rows), 0 : 2 * ROWS].T
            found = found[0:ROWS] + found[ROWS : 2 * ROWS]
            found = jnp.where(iota((ROWS, rows), 1) < count, found, 0.0)
            out_ref[r, :, 0:rows] = jnp.where(row == 6, sums_ref[:, 0:rows], found)
            if rows < width:
                out_ref[r, :, rows:width] = jnp.zeros((ROWS, width - rows), F32)

    by_width(longest, width, run)


def unpack_kernel(where_ref, segs_ref, partial_ref, out_ref):
    _, place = near_rank(segs_ref[6:7, :], where_ref[1])
    total = jnp.sum(partial_ref[...], axis=0)
    spreaded = jnp.dot(total, place, precision=HIGH, preferred_element_type=F32)
    total = jnp.where(iota(total.shape, 0) == 6, total, spreaded)
    out_ref[...] = jnp.broadcast_to(total[None], out_ref.shape)


def finish_kernel(scale, partial_ref, b_ref, u_ref, correction_ref, stress_ref):
    total = jnp.sum(partial_ref[...], axis=0)
    bb, bu, uu, uau = [total[6:7, i : i + 1] for i in range(4)]
    alpha = bb / bu
    later = bb - 2.0 * alpha * bu + alpha * alpha * uu
    beta = later / bb
    grow = 1.0 + beta
    alpha_next = later / (grow * grow * bu - 2.0 * alpha * grow * uu + alpha * alpha * uau)
    on_b = alpha + alpha_next * grow
    on_u = -alpha_next * alpha
    stress_ref[...] = (on_b * total[0:3] + on_u * total[3:6]) * scale
    for c in range(3):
        correction_ref[c] = on_b * b_ref[c] + on_u * u_ref[c]


def call(kernel, out, scratch=(), smem=0, inputs=0, flops=0, moved=0):
    vmem = pl.BlockSpec(memory_space=pltpu.VMEM)
    ints = pl.BlockSpec(memory_space=pltpu.SMEM)
    shapes, specs = [], []
    for o in out:
        whole = isinstance(o, jax.ShapeDtypeStruct)
        shapes.append(o if whole else jax.ShapeDtypeStruct(o, F32))
        specs.append(ints if whole and o.dtype == jnp.int32 else vmem)
    single = len(shapes) == 1
    return pl.pallas_call(
        kernel,
        out_shape=shapes[0] if single else tuple(shapes),
        in_specs=[ints] * smem + [vmem] * inputs,
        out_specs=specs[0] if single else tuple(specs),
        scratch_shapes=list(scratch),
        compiler_params=pltpu.CompilerParams(vmem_limit_bytes=VMEM_LIMIT),
        cost_estimate=pl.CostEstimate(flops=flops, bytes_accessed=moved, transcendentals=0),
    )


def shards(seg_pos, burgers, seg_tile, quad_pos, quad_node, stiffness):
    n_seg, n_fe = lax.axis_size("seg"), lax.axis_size("fe")
    column, block = lax.axis_index("seg"), lax.axis_index("fe")
    s_dev = seg_pos.shape[1]
    q_block = quad_pos.shape[1]
    q_dev = q_block // n_seg
    total_segs = s_dev * n_seg
    total_points = q_block * n_fe
    wide, tall, deep = stiffness.shape
    rows = wide * tall
    where = jnp.stack([column, block]).astype(jnp.int32)
    tile = seg_tile.reshape(1, s_dev).astype(F32)
    segs = jnp.concatenate([seg_pos, burgers, tile, tile], axis=0)
    nodes = quad_node.reshape(q_block // LANES, LANES)
    points = lax.dynamic_slice_in_dim(quad_pos, column * q_dev, q_dev, 1)
    stiff = stiffness.reshape(rows, deep)

    up_seg = [(i, (i + 1) % n_seg) for i in range(n_seg)]
    down_seg = [((i + 1) % n_seg, i) for i in range(n_seg)]
    up_fe = [(i, (i + 1) % n_fe) for i in range(n_fe)]
    down_fe = [((i + 1) % n_fe, i) for i in range(n_fe)]
    field, line = (3, rows, deep), (ROWS, q_dev)
    face, message = (ROWS, rows), (ROWS, rows + 2 * LANES)
    long = total_segs + 2 * CHUNK
    sbuf = pltpu.VMEM((long, LANES), F32)
    spreaded = pltpu.VMEM((3, CHUNK, LANES), F32)
    cols = pltpu.VMEM((6 * LANES, q_dev), BF16)

    packed = call(pack_kernel, [(n_seg, ROWS, s_dev)], smem=1, inputs=1)(where, segs)
    groups = lax.all_to_all(packed, "seg", 0, 0, tiled=True)
    kq, kz, hot = call(
        prepare_kernel, [line, face, jax.ShapeDtypeStruct((rows + LANES, q_dev), BF16)],
        [pltpu.VMEM((LANES, 2 * rows), BF16)], smem=1, inputs=2, flops=10**9, moved=10**6,
    )(where, nodes, stiff)

    def traction(*refs):
        traction_kernel(STRENGTH / math.sqrt(total_segs), *refs)

    weights = jax.ShapeDtypeStruct((KEPT + 1, 2, CHUNK, q_dev), BF16)
    t, sent, kept = call(
        traction, [line, (ROWS, q_dev // 2), weights], [sbuf, spreaded, pltpu.VMEM((2 * ROWS, q_dev), F32)], inputs=3,
        flops=10**10, moved=10**6,
    )(groups, points, kq)
    from_left = lax.ppermute(sent, "seg", up_seg)
    from_right = lax.ppermute(sent, "seg", down_seg)

    def scatter(*refs):
        scatter_kernel(n_seg, *refs)

    side_hot = jax.ShapeDtypeStruct((5 * LANES, q_dev), BF16)
    b, g, low, after, high, side_hot = call(
        scatter, [field, line, face, face, face, side_hot], [cols, pltpu.VMEM((3 * LANES, 2 * rows), BF16)],
        smem=1, inputs=3, flops=4 * 10**9, moved=4 * 10**6,
    )(where, nodes, t, hot)

    def fill_sides(*refs):
        sides_kernel(n_seg, *refs)

    sides, down, up = call(
        fill_sides, [(12, tall, deep), message, message], [cols],
        smem=1, inputs=7, flops=2 * 10**9, moved=10**6,
    )(where, from_left, from_right, side_hot, low, after, high, kz)
    above = lax.ppermute(down, "fe", down_fe)
    below = lax.ppermute(up, "fe", up_fe)
    u, ur, g, uh = call(
        operate_kernel, [field, (3, tall, deep), line, face], [pltpu.VMEM((3 * LANES, 2 * rows), BF16)],
        smem=1, inputs=6, flops=4 * 10**9, moved=4 * 10**6,
    )(where, nodes, b, sides, stiff, g, hot)

    def fill_ends(*refs):
        ends_kernel(n_seg, n_fe, *refs)

    u, motion, sums = call(
        fill_ends, [field, line, (ROWS, LANES)], smem=1, inputs=11, flops=10**9, moved=4 * 10**6
    )(where, nodes, b, u, ur, stiff, above, below, uh, high, g, hot)
    partial = call(
        stress_kernel, [(n_seg, ROWS, s_dev)],
        [sbuf, spreaded, pltpu.VMEM((long, LANES), F32), pltpu.VMEM((2 * ROWS, q_dev), BF16)],
        inputs=5, flops=10**10, moved=10**6,
    )(groups, kept, points, motion, sums)
    partial = lax.all_to_all(partial, "seg", 0, 0, tiled=True)
    partial = call(unpack_kernel, [(n_fe, ROWS, s_dev)], smem=1, inputs=2)(where, segs, partial)
    partial = lax.all_to_all(partial, "fe", 0, 0, tiled=True)

    def finish(*refs):
        finish_kernel(4.0 * STRENGTH / math.sqrt(total_points), *refs)

    correction, stress = call(finish, [(3, rows, deep), (3, s_dev)], inputs=3)(partial, b, u)
    return correction.reshape(3, wide, tall, deep), stress


def solution(mesh):
    placed = (
        P(None, "seg"),
        P(None, "seg"),
        P("seg"),
        P(None, "fe"),
        P("fe"),
        P("seg", None, "fe"),
    )
    return jax.shard_map(
        shards,
        mesh=mesh,
        in_specs=placed,
        out_specs=(P(None, "seg", None, "fe"), P(None, "seg")),
        check_vma=False,
    )
```

```python
import math

import jax
import jax.numpy as jnp
from jax import lax
from jax.experimental import pallas as pl
from jax.experimental.pallas import tpu as pltpu
from jax.sharding import PartitionSpec as P

CORE = 0.0001
STRENGTH = 0.001
HIGH = lax.Precision.HIGHEST
F32 = jnp.float32
BF16 = jnp.bfloat16
ROWS = 8
LANES = 128
CHUNK = 256
KEPT = 7
NT = (((1,), (1,)), ((), ()))
VMEM_LIMIT = 12 * 1024 * 1024


def iota(shape, dim):
    return lax.broadcasted_iota(jnp.int32, shape, dim)


def split(x):
    hi = x.astype(BF16)
    return hi, (x - hi.astype(F32)).astype(BF16)


def near_rank(tile, block):
    near = jnp.abs(tile - block) <= 1
    mask = jnp.where(near, 1.0, 0.0)
    n = tile.shape[1]
    before = jnp.where(iota((n, n), 0) < iota((n, n), 1), 1.0, 0.0)
    rank = jnp.dot(jnp.broadcast_to(mask, (ROWS, n)), before, preferred_element_type=F32)[:1]
    place = jnp.where(iota((n, n), 0) == rank.astype(jnp.int32), mask, 0.0)
    return mask, place


def pack_kernel(where_ref, segs_ref, tile_ref, out_ref):
    mask, place = near_rank(tile_ref[...], where_ref[1])
    rest = jnp.broadcast_to(mask, (2, mask.shape[1]))
    segs = jnp.concatenate([segs_ref[...], rest], axis=0)
    packed = lax.dot_general(segs, place, NT, precision=HIGH, preferred_element_type=F32)
    out_ref[...] = jnp.broadcast_to(packed[None], out_ref.shape)


def measured(groups_ref):
    offset, longest = 0, 0
    places = []
    for r in range(groups_ref.shape[0]):
        count = jnp.sum(groups_ref[r, 6:7, :]).astype(jnp.int32)
        places.append((offset, count))
        offset = offset + count
        longest = jnp.maximum(longest, count)
    return places, offset, longest


def by_width(longest, width, run):
    half = width // 2

    @pl.when(longest <= half)
    def _():
        run(half)

    @pl.when(longest > half)
    def _():
        run(width)


def assemble(groups_ref, sbuf):
    places, total, longest = measured(groups_ref)

    def run(rows):
        for r, (offset, _) in enumerate(places):
            sbuf[pl.ds(offset, rows), 0:ROWS] = groups_ref[r].T[0:rows]

    by_width(longest, groups_ref.shape[2], run)
    sbuf[pl.ds(total, CHUNK), 0:ROWS] = jnp.zeros((CHUNK, ROWS), F32)
    return places, total, longest


def in_chunks(total, chunk):
    quarter, half = CHUNK // 4, CHUNK // 2
    whole = total // CHUNK
    rest = total - whole * CHUNK
    n = whole + jnp.where(rest > half, 1, 0)

    def step(i, carry):
        chunk(pl.multiple_of(i * CHUNK, CHUNK), CHUNK)
        return carry

    lax.fori_loop(0, n, step, jnp.int32(0))
    for least, most in ((0, quarter), (quarter, half)):

        @pl.when(jnp.logical_and(rest > least, rest <= most))
        def _():
            chunk(pl.multiple_of(whole * CHUNK, CHUNK), most)


def spread(sbuf, wide, start, size):
    for d in range(3):
        wide[d, 0:size] = jnp.broadcast_to(sbuf[pl.ds(start, size), d : d + 1], (size, LANES))


def cubes(wide, q_ref, start, size):
    his, los = [], []
    for j in range(CHUNK // LANES):
        at = pl.ds(pl.multiple_of(start + j * LANES, LANES), LANES)
        dx = wide[0, 0:size] - q_ref[0:1, at]
        dy = wide[1, 0:size] - q_ref[1:2, at]
        dz = wide[2, 0:size] - q_ref[2:3, at]
        inverse = lax.rsqrt((dx * dx + CORE) + (dy * dy + dz * dz))
        hi, lo = split(inverse * inverse * inverse)
        his.append(hi)
        los.append(lo)
    return jnp.concatenate(his, axis=1), jnp.concatenate(los, axis=1)


def traction_kernel(scale, groups_ref, q_ref, kq_ref, out_ref, sent_ref, kept_ref, sbuf, wide, total):
    q_dev = q_ref.shape[1]
    _, length, _ = assemble(groups_ref, sbuf)
    total[...] = jnp.zeros_like(total)

    def chunk(start, size):
        spread(sbuf, wide, start, size)
        vectors = jnp.concatenate(split(sbuf[pl.ds(start, size), 0:ROWS].T), axis=0)
        vectors = jnp.concatenate([vectors, vectors], axis=1)
        slot = jnp.minimum(start // CHUNK, KEPT)

        def block(j, c):
            at = pl.multiple_of(j * CHUNK, CHUNK)
            hi, lo = cubes(wide, q_ref, at, size)
            kept_ref[slot, 0, 0:size, pl.ds(at, CHUNK)] = hi
            kept_ref[slot, 1, 0:size, pl.ds(at, CHUNK)] = lo
            weights = jnp.concatenate([hi, lo], axis=0)
            total[:, pl.ds(at, CHUNK)] += jnp.dot(vectors, weights, preferred_element_type=F32)
            return c

        lax.fori_loop(0, q_dev // CHUNK, block, jnp.int32(0), unroll=8)

    in_chunks(length, chunk)
    both = (total[0:ROWS, :] + total[ROWS : 2 * ROWS, :]) * scale
    out_ref[...] = jnp.zeros_like(out_ref)
    out_ref[0:3, :] = both[3:6, :]
    half = q_dev // 2
    for p in range(2):
        at = slice(p * half, (p + 1) * half)
        sent_ref[4 * p : 4 * p + 3, :] = both[3:6, at]
        sent_ref[4 * p + 3 : 4 * p + 4, :] = kq_ref[0:1, at]


def nodes_of(nodes_ref, r, n):
    return nodes_ref[pl.ds(pl.multiple_of(r * n, n), n), :]


def set_hot(nodes, out_ref, first):
    rows = out_ref.shape[0]
    for k in range(nodes.shape[0]):
        row = nodes[k : k + 1, :] // LANES - first
        here = jnp.where(iota((rows, LANES), 0) == row, 1.0, 0.0)
        out_ref[:, k * LANES : (k + 1) * LANES] = here.astype(BF16)


def set_spot(nodes, out_ref):
    for k in range(nodes.shape[0]):
        here = jnp.where(iota((LANES, LANES), 0) == nodes[k : k + 1, :] % LANES, 1.0, 0.0)
        out_ref[:, k * LANES : (k + 1) * LANES] = here.astype(BF16)


def spread_points(spot_ref, values, cols):
    n = spot_ref.shape[1]
    for p, parts in enumerate(split(values)):
        for c in range(3):
            to = (p * 3 + c) * LANES
            for k in range(0, n, CHUNK):
                at = slice(k, k + CHUNK)
                part = jnp.broadcast_to(parts[c : c + 1, at], (LANES, CHUNK))
                cols[to : to + LANES, at] = spot_ref[:, at] * part


def layers(hot, cols):
    out = lax.dot_general(hot, cols, NT, preferred_element_type=F32)
    half = 3 * LANES
    return out[:, :half] + out[:, half:]


def set_parts(parts, place, x, rows, tile):
    hi, lo = split(tile)
    to = slice(place * LANES, (place + 1) * LANES)
    parts[to, x * LANES : (x + 1) * LANES] = hi
    parts[to, rows + x * LANES : rows + (x + 1) * LANES] = lo


def pair(nodes, k):
    return jnp.concatenate([nodes[k : k + 1, :], nodes[k + 1 : k + 2, :]], axis=1)


def gather(nodes, hot_ref, parts, fields, out_ref, first):
    for k in range(0, nodes.shape[0], 2):
        at = slice(k * LANES, (k + 2) * LANES)
        here = hot_ref[0 : parts.shape[1] // 2, at]
        found = jnp.dot(parts[...], jnp.concatenate([here, here], axis=0), preferred_element_type=F32)
        pick = iota((LANES, 2 * LANES), 0) == pair(nodes, k) % LANES
        for f in range(fields):
            value = jnp.where(pick, found[f * LANES : (f + 1) * LANES, :], 0.0)
            out_ref[first + f : first + f + 1, at] = jnp.sum(value, axis=0, keepdims=True)


def prepare_kernel(where_ref, nodes_ref, k_ref, kq_ref, kz_ref, hot_ref, parts):
    rows = k_ref.shape[0]
    n = kq_ref.shape[1] // LANES
    nodes = nodes_of(nodes_ref, where_ref[0], n)
    set_hot(nodes, hot_ref.at[0:rows], 0)
    set_spot(nodes, hot_ref.at[rows : rows + LANES])
    kz_ref[...] = jnp.zeros_like(kz_ref)
    for x in range(rows // LANES):
        at = slice(x * LANES, (x + 1) * LANES)
        tile = k_ref[at, :].T
        kz_ref[0:1, at] = tile[0:1, :]
        set_parts(parts, 0, x, rows, tile)
    kq_ref[...] = jnp.zeros_like(kq_ref)
    gather(nodes, hot_ref, parts, 1, kq_ref, 0)


def scatter_kernel(
    where_ref, nodes_ref, t_ref, hot_ref, b_ref, g_ref, low_ref, next_ref, high_ref, cols, parts
):
    n = t_ref.shape[1] // LANES
    rows = b_ref.shape[1]
    spread_points(hot_ref.at[rows : rows + LANES], t_ref[...], cols)
    load = layers(hot_ref[0:rows, :], cols[...])
    for ref in (low_ref, next_ref, high_ref):
        ref[...] = jnp.zeros_like(ref)
    for c in range(3):
        for x in range(rows // LANES):
            at = slice(x * LANES, (x + 1) * LANES)
            f = load[at, c * LANES : (c + 1) * LANES]
            b_ref[c, at, :] = f
            tile = f.T
            set_parts(parts, c, x, rows, tile)
            low_ref[c : c + 1, at] = tile[0:1, :]
            next_ref[c : c + 1, at] = tile[1:2, :]
            high_ref[c : c + 1, at] = tile[LANES - 1 : LANES, :]
    g_ref[...] = jnp.zeros_like(g_ref)
    gather(nodes_of(nodes_ref, where_ref[0], n), hot_ref, parts, 3, g_ref, 0)


def unfold(sent):
    return jnp.concatenate([sent[0:4], sent[4:8]], axis=1)


def sides_kernel(
    n_seg, where_ref, nodes_ref, left_ref, right_ref, low_ref, next_ref, high_ref, kz_ref,
    sides_ref, down_ref, up_ref, hot, spot, cols,
):
    n = hot.shape[1] // LANES
    rows = low_ref.shape[1]
    me = where_ref[0]
    down_ref[...] = jnp.zeros_like(down_ref)
    up_ref[...] = jnp.zeros_like(up_ref)
    own = slice(LANES, LANES + rows)
    down_ref[0:3, own] = low_ref[0:3, :]
    down_ref[3:6, own] = next_ref[0:3, :]
    down_ref[6:7, own] = kz_ref[0:1, :]
    up_ref[0:3, own] = high_ref[0:3, :]

    nodes = nodes_of(nodes_ref, jnp.maximum(me - 1, 0), n)
    set_hot(nodes, hot.at[0:LANES], rows - LANES)
    set_spot(nodes, spot)
    spread_points(spot, unfold(left_ref[...]) * jnp.where(me > 0, 1.0, 0.0), cols)
    left = layers(hot[0:LANES, :], cols[...])
    nodes = nodes_of(nodes_ref, jnp.minimum(me + 1, n_seg - 1), n)
    set_hot(nodes, hot, 0)
    set_spot(nodes, spot)
    t = unfold(right_ref[...])
    kq = t[3:4]
    t = t * jnp.where(me < n_seg - 1, 1.0, 0.0)
    spread_points(spot, t, cols)
    right = layers(hot[...], cols[...])
    spread_points(spot, t * kq, cols)
    stiff = layers(hot[0:LANES, :], cols[...])
    last = slice(LANES + rows, 2 * LANES + rows)
    for c in range(3):
        comp = slice(c * LANES, (c + 1) * LANES)
        sides_ref[c] = left[:, comp]
        sides_ref[3 + c] = right[0:LANES, comp]
        sides_ref[6 + c] = right[LANES : 2 * LANES, comp]
        sides_ref[9 + c] = stiff[:, comp]
        down_ref[c : c + 1, 0:LANES] = left[:, comp].T[0:1, :]
        tile = right[0:LANES, comp].T
        down_ref[c : c + 1, last] = tile[0:1, :]
        up_ref[c : c + 1, last] = tile[LANES - 1 : LANES, :]


def beside_in_layer(f):
    i, j = iota(f.shape, 0), iota(f.shape, 1)
    n, m = f.shape
    up = jnp.where(i == 0, 0.0, pltpu.roll(f, 1, 0)) + jnp.where(i == n - 1, 0.0, pltpu.roll(f, n - 1, 0))
    return up + (jnp.where(j == 0, 0.0, pltpu.roll(f, 1, 1)) + jnp.where(j == m - 1, 0.0, pltpu.roll(f, m - 1, 1)))


def operate_kernel(
    where_ref, nodes_ref, b_ref, sides_ref, k_ref, g_ref, hot_ref, u_ref, ur_ref, motion_ref, high_ref, parts
):
    n = g_ref.shape[1] // LANES
    rows = b_ref.shape[1]
    wide = rows // LANES
    high_ref[...] = jnp.zeros_like(high_ref)
    for c in range(3):
        b4 = sides_ref[3 + c]
        field = [sides_ref[c]] + [b_ref[c, x * LANES : (x + 1) * LANES, :] for x in range(wide)] + [b4]
        for x in range(wide):
            at = slice(x * LANES, (x + 1) * LANES)
            f = field[x + 1]
            u = (6.0 + k_ref[at, :]) * f - (beside_in_layer(f) + (field[x] + field[x + 2]))
            u_ref[c, at, :] = u
            tile = u.T
            high_ref[c : c + 1, at] = tile[LANES - 1 : LANES, :]
            set_parts(parts, c, x, rows, tile)
        ur_ref[c] = 6.0 * b4 + sides_ref[9 + c] - (field[wide] + sides_ref[6 + c] + beside_in_layer(b4))
    motion_ref[...] = g_ref[...]
    gather(nodes_of(nodes_ref, where_ref[0], n), hot_ref, parts, 3, motion_ref, 3)


def ends_kernel(
    n_seg, n_fe, where_ref, nodes_ref, b_ref, u_ref, ur_ref, k_ref, above_ref, below_ref, uh_ref, high_ref, g_ref,
    hot_ref, out_ref, motion_ref, sums_ref,
):
    n = g_ref.shape[1] // LANES
    rows = b_ref.shape[1]
    wide = rows // LANES
    me, block = where_ref[0], where_ref[1]
    is_above = jnp.where(block < n_fe - 1, 1.0, 0.0)
    above = above_ref[...] * is_above
    below = below_ref[...] * jnp.where(block > 0, 1.0, 0.0)
    own = slice(LANES, LANES + rows)

    center = above[0:3, own]
    place = iota(center.shape, 1) % LANES
    beside = above[0:3, 0:rows] + above[0:3, 2 * LANES : 2 * LANES + rows]
    beside = beside + jnp.where(place == 0, 0.0, pltpu.roll(center, 1, 1))
    beside = beside + jnp.where(place == LANES - 1, 0.0, pltpu.roll(center, rows - 1, 1))
    beside = beside + high_ref[0:3, :] + above[3:6, own]
    next_u = (6.0 + above[6:7, own]) * center - beside
    crossing = is_above * jnp.sum((uh_ref[0:3, :] - center) * next_u)

    above_t, below_t = above.T, below.T
    lane = iota((LANES, LANES), 1)
    zero = jnp.zeros((LANES, LANES), F32)
    bb, bu, uu, uau = zero, zero, zero, zero
    not_last = jnp.where(me < n_seg - 1, 2.0, 0.0)

    def ends(c, x):
        at = slice((x + 1) * LANES, (x + 2) * LANES)
        low = jnp.where(lane == 0, below_t[at, c : c + 1], 0.0)
        return low + jnp.where(lane == LANES - 1, above_t[at, c : c + 1], 0.0)

    for c in range(3):
        us = []
        for x in range(wide):
            at = slice(x * LANES, (x + 1) * LANES)
            f = b_ref[c, at, :]
            u = u_ref[c, at, :] - ends(c, x)
            out_ref[c, at, :] = u
            us.append(u)
            bb = bb + f * f
            bu = bu + f * u
            uu = uu + u * u
        us.append(not_last * (ur_ref[c] - ends(c, wide)))
        for x in range(wide):
            at = slice(x * LANES, (x + 1) * LANES)
            beside = beside_in_layer(us[x]) + (us[x + 1] if x + 1 == wide else 2.0 * us[x + 1])
            uau = uau + us[x] * ((6.0 + k_ref[at, :]) * us[x] - beside)
    line = iota((1, LANES), 1)
    sums = jnp.where(line == 3, -2.0 * crossing, 0.0)
    for i, part in enumerate((bb, bu, uu, uau)):
        sums = sums + jnp.where(line == i, jnp.sum(part), 0.0)
    sums_ref[...] = jnp.broadcast_to(sums, sums_ref.shape)

    nodes = nodes_of(nodes_ref, me, n)
    faces = jnp.concatenate(split(below[:, own]) + split(above[:, own]), axis=0)
    motion_ref[...] = g_ref[...]
    for k in range(0, n, 2):
        at = slice(k * LANES, (k + 2) * LANES)
        found = jnp.dot(faces, hot_ref[0:rows, at], preferred_element_type=F32)
        last = pair(nodes, k) % LANES
        extra = jnp.where(last == 0, found[0:3] + found[8:11], 0.0)
        extra = extra + jnp.where(last == LANES - 1, found[16:19] + found[24:27], 0.0)
        motion_ref[3:6, at] = g_ref[3:6, at] - extra


def stress_kernel(groups_ref, kept_ref, q_ref, g_ref, sums_ref, out_ref, sbuf, wide, results, motion):
    q_dev = q_ref.shape[1]
    n_groups, _, width = out_ref.shape
    places, length, longest = measured(groups_ref)
    motion[...] = jnp.concatenate(split(g_ref[...]), axis=0)
    n_chunks = (length + (CHUNK - 1)) // CHUNK

    def from_kept(start, size):
        i = start // CHUNK
        m = motion[...]
        found = lax.dot_general(kept_ref[i, 0, 0:size], m, NT, preferred_element_type=F32)
        found = found + lax.dot_general(kept_ref[i, 1, 0:size], m, NT, preferred_element_type=F32)
        results[pl.ds(start, size), 0 : 2 * ROWS] = found

    in_chunks(jnp.minimum(length, KEPT * CHUNK), from_kept)

    def again(i, carry):
        start = pl.multiple_of(i * CHUNK, CHUNK)
        spread(sbuf, wide, start, CHUNK)

        def block(j, total):
            at = pl.multiple_of(j * CHUNK, CHUNK)
            hi, lo = cubes(wide, q_ref, at, CHUNK)
            m = motion[:, pl.ds(at, CHUNK)]
            total = total + lax.dot_general(hi, m, NT, preferred_element_type=F32)
            return total + lax.dot_general(lo, m, NT, preferred_element_type=F32)

        results[pl.ds(start, CHUNK), 0 : 2 * ROWS] = lax.fori_loop(
            0, q_dev // CHUNK, block, jnp.zeros((CHUNK, 2 * ROWS), F32), unroll=8
        )
        return carry

    @pl.when(n_chunks > KEPT)
    def _():
        assemble(groups_ref, sbuf)
        lax.fori_loop(KEPT, n_chunks, again, jnp.int32(0))

    def run(rows):
        row = iota((ROWS, rows), 0)
        for r, (offset, count) in enumerate(places):
            found = results[pl.ds(offset, rows), 0 : 2 * ROWS].T
            found = found[0:ROWS] + found[ROWS : 2 * ROWS]
            found = jnp.where(iota((ROWS, rows), 1) < count, found, 0.0)
            out_ref[r, :, 0:rows] = jnp.where(row == 6, sums_ref[:, 0:rows], found)
            if rows < width:
                out_ref[r, :, rows:width] = jnp.zeros((ROWS, width - rows), F32)

    by_width(longest, width, run)


def unpack_kernel(where_ref, tile_ref, partial_ref, out_ref):
    _, place = near_rank(tile_ref[...], where_ref[1])
    total = jnp.sum(partial_ref[...], axis=0)
    spreaded = jnp.dot(total, place, precision=HIGH, preferred_element_type=F32)
    total = jnp.where(iota(total.shape, 0) == 6, total, spreaded)
    out_ref[...] = jnp.broadcast_to(total[None], out_ref.shape)


def finish_kernel(scale, partial_ref, b_ref, u_ref, correction_ref, stress_ref):
    total = jnp.sum(partial_ref[...], axis=0)
    bb, bu, uu, uau = [total[6:7, i : i + 1] for i in range(4)]
    alpha = bb / bu
    later = bb - 2.0 * alpha * bu + alpha * alpha * uu
    beta = later / bb
    grow = 1.0 + beta
    alpha_next = later / (grow * grow * bu - 2.0 * alpha * grow * uu + alpha * alpha * uau)
    on_b = alpha + alpha_next * grow
    on_u = -alpha_next * alpha
    stress_ref[...] = (on_b * total[0:3] + on_u * total[3:6]) * scale
    for c in range(3):
        correction_ref[c] = on_b * b_ref[c] + on_u * u_ref[c]


def call(kernel, out, scratch=(), smem=0, inputs=0, flops=0, moved=0):
    vmem = pl.BlockSpec(memory_space=pltpu.VMEM)
    ints = pl.BlockSpec(memory_space=pltpu.SMEM)
    shapes = []
    for o in out:
        shapes.append(o if isinstance(o, jax.ShapeDtypeStruct) else jax.ShapeDtypeStruct(o, F32))
    single = len(shapes) == 1
    return pl.pallas_call(
        kernel,
        out_shape=shapes[0] if single else tuple(shapes),
        in_specs=[ints] * smem + [vmem] * inputs,
        out_specs=vmem if single else (vmem,) * len(shapes),
        scratch_shapes=list(scratch),
        compiler_params=pltpu.CompilerParams(vmem_limit_bytes=VMEM_LIMIT),
        cost_estimate=pl.CostEstimate(flops=flops, bytes_accessed=moved, transcendentals=0),
    )


def shards(seg_pos, burgers, seg_tile, quad_pos, quad_node, stiffness):
    n_seg, n_fe = lax.axis_size("seg"), lax.axis_size("fe")
    column, block = lax.axis_index("seg"), lax.axis_index("fe")
    s_dev = seg_pos.shape[1]
    q_block = quad_pos.shape[1]
    q_dev = q_block // n_seg
    total_segs = s_dev * n_seg
    total_points = q_block * n_fe
    wide, tall, deep = stiffness.shape
    rows = wide * tall
    where = jnp.stack([column, block]).astype(jnp.int32)
    tile = seg_tile.reshape(1, s_dev)
    nodes = quad_node.reshape(q_block // LANES, LANES)
    points = lax.dynamic_slice_in_dim(quad_pos, column * q_dev, q_dev, 1)
    stiff = stiffness.reshape(rows, deep)

    up_seg = [(i, (i + 1) % n_seg) for i in range(n_seg)]
    down_seg = [((i + 1) % n_seg, i) for i in range(n_seg)]
    up_fe = [(i, (i + 1) % n_fe) for i in range(n_fe)]
    down_fe = [((i + 1) % n_fe, i) for i in range(n_fe)]
    field, line = (3, rows, deep), (ROWS, q_dev)
    face, message = (ROWS, rows), (ROWS, rows + 2 * LANES)
    long = total_segs + 2 * CHUNK
    sbuf = pltpu.VMEM((long, LANES), F32)
    spreaded = pltpu.VMEM((3, CHUNK, LANES), F32)
    cols = pltpu.VMEM((6 * LANES, q_dev), BF16)

    segs = jnp.concatenate([seg_pos, burgers], axis=0)
    packed = call(pack_kernel, [(n_seg, ROWS, s_dev)], smem=1, inputs=2)(where, segs, tile)
    groups = lax.all_to_all(packed, "seg", 0, 0, tiled=True)
    kq, kz, hot = call(
        prepare_kernel, [line, face, jax.ShapeDtypeStruct((rows + LANES, q_dev), BF16)],
        [pltpu.VMEM((LANES, 2 * rows), BF16)], smem=1, inputs=2, flops=10**9, moved=10**6,
    )(where, nodes, stiff)

    def traction(*refs):
        traction_kernel(STRENGTH / math.sqrt(total_segs), *refs)

    weights = jax.ShapeDtypeStruct((KEPT + 1, 2, CHUNK, q_dev), BF16)
    t, sent, kept = call(
        traction, [line, (ROWS, q_dev // 2), weights], [sbuf, spreaded, pltpu.VMEM((2 * ROWS, q_dev), F32)], inputs=3,
        flops=10**10, moved=10**6,
    )(groups, points, kq)
    from_left = lax.ppermute(sent, "seg", up_seg)
    from_right = lax.ppermute(sent, "seg", down_seg)

    b, g, low, after, high = call(
        scatter_kernel, [field, line, face, face, face], [cols, pltpu.VMEM((3 * LANES, 2 * rows), BF16)],
        smem=1, inputs=3, flops=4 * 10**9, moved=4 * 10**6,
    )(where, nodes, t, hot)

    def fill_sides(*refs):
        sides_kernel(n_seg, *refs)

    sides, down, up = call(
        fill_sides, [(12, tall, deep), message, message],
        [pltpu.VMEM((2 * LANES, q_dev), BF16), pltpu.VMEM((LANES, q_dev), BF16), cols],
        smem=1, inputs=7, flops=2 * 10**9, moved=10**6,
    )(where, nodes, from_left, from_right, low, after, high, kz)
    above = lax.ppermute(down, "fe", down_fe)
    below = lax.ppermute(up, "fe", up_fe)
    u, ur, g, uh = call(
        operate_kernel, [field, (3, tall, deep), line, face], [pltpu.VMEM((3 * LANES, 2 * rows), BF16)],
        smem=1, inputs=6, flops=4 * 10**9, moved=4 * 10**6,
    )(where, nodes, b, sides, stiff, g, hot)

    def fill_ends(*refs):
        ends_kernel(n_seg, n_fe, *refs)

    u, motion, sums = call(
        fill_ends, [field, line, (ROWS, LANES)], smem=1, inputs=11, flops=10**9, moved=4 * 10**6
    )(where, nodes, b, u, ur, stiff, above, below, uh, high, g, hot)
    partial = call(
        stress_kernel, [(n_seg, ROWS, s_dev)],
        [sbuf, spreaded, pltpu.VMEM((long, LANES), F32), pltpu.VMEM((2 * ROWS, q_dev), BF16)],
        inputs=5, flops=10**10, moved=10**6,
    )(groups, kept, points, motion, sums)
    partial = lax.all_to_all(partial, "seg", 0, 0, tiled=True)
    partial = call(unpack_kernel, [(n_fe, ROWS, s_dev)], smem=1, inputs=2)(where, tile, partial)
    partial = lax.all_to_all(partial, "fe", 0, 0, tiled=True)

    def finish(*refs):
        finish_kernel(4.0 * STRENGTH / math.sqrt(total_points), *refs)

    correction, stress = call(finish, [(3, rows, deep), (3, s_dev)], inputs=3)(partial, b, u)
    return correction.reshape(3, wide, tall, deep), stress


def solution(mesh):
    placed = (
        P(None, "seg"),
        P(None, "seg"),
        P("seg"),
        P(None, "fe"),
        P("fe"),
        P("seg", None, "fe"),
    )
    return jax.shard_map(
        shards,
        mesh=mesh,
        in_specs=placed,
        out_specs=(P(None, "seg", None, "fe"), P(None, "seg")),
        check_vma=False,
    )
```

```python
import math

import jax
import jax.numpy as jnp
from jax import lax
from jax.experimental import pallas as pl
from jax.experimental.pallas import tpu as pltpu
from jax.sharding import PartitionSpec as P

CORE = 0.0001
STRENGTH = 0.001
HIGH = lax.Precision.HIGHEST
F32 = jnp.float32
BF16 = jnp.bfloat16
ROWS = 8
LANES = 128
CHUNK = 256
KEPT = 7
NT = (((1,), (1,)), ((), ()))
VMEM_LIMIT = 12 * 1024 * 1024
PACK_LIMIT = 60 * 1024 * 1024


def iota(shape, dim):
    return lax.broadcasted_iota(jnp.int32, shape, dim)


def split(x):
    hi = x.astype(BF16)
    return hi, (x - hi.astype(F32)).astype(BF16)


def near_rank(tile, block):
    near = jnp.abs(tile - block) <= 1
    mask = jnp.where(near, 1.0, 0.0)
    n = tile.shape[1]
    before = jnp.where(iota((n, n), 0) < iota((n, n), 1), 1.0, 0.0)
    rank = jnp.dot(jnp.broadcast_to(mask, (ROWS, n)), before, preferred_element_type=F32)[:1]
    place = jnp.where(iota((n, n), 0) == rank.astype(jnp.int32), mask, 0.0)
    return mask, place


def pack_kernel(where_ref, pos_ref, burgers_ref, tile_ref, out_ref):
    mask, place = near_rank(tile_ref[...], where_ref[1])
    rest = jnp.broadcast_to(mask, (2, mask.shape[1]))
    segs = jnp.concatenate([pos_ref[...], burgers_ref[...], rest], axis=0)
    packed = lax.dot_general(segs, place, NT, precision=HIGH, preferred_element_type=F32)
    out_ref[...] = jnp.broadcast_to(packed[None], out_ref.shape)


def measured(groups_ref):
    offset, longest = 0, 0
    places = []
    for r in range(groups_ref.shape[0]):
        count = jnp.sum(groups_ref[r, 6:7, :]).astype(jnp.int32)
        places.append((offset, count))
        offset = offset + count
        longest = jnp.maximum(longest, count)
    return places, offset, longest


def by_width(longest, width, run):
    half = width // 2

    @pl.when(longest <= half)
    def _():
        run(half)

    @pl.when(longest > half)
    def _():
        run(width)


def assemble(groups_ref, sbuf):
    places, total, longest = measured(groups_ref)

    def run(rows):
        for r, (offset, _) in enumerate(places):
            sbuf[pl.ds(offset, rows), 0:ROWS] = groups_ref[r].T[0:rows]

    by_width(longest, groups_ref.shape[2], run)
    sbuf[pl.ds(total, CHUNK), 0:ROWS] = jnp.zeros((CHUNK, ROWS), F32)
    return places, total, longest


def in_chunks(total, chunk):
    quarter, half = CHUNK // 4, CHUNK // 2
    whole = total // CHUNK
    rest = total - whole * CHUNK
    n = whole + jnp.where(rest > half, 1, 0)

    def step(i, carry):
        chunk(pl.multiple_of(i * CHUNK, CHUNK), CHUNK)
        return carry

    lax.fori_loop(0, n, step, jnp.int32(0))
    for least, most in ((0, quarter), (quarter, half)):

        @pl.when(jnp.logical_and(rest > least, rest <= most))
        def _():
            chunk(pl.multiple_of(whole * CHUNK, CHUNK), most)


def spread(sbuf, wide, start, size):
    for d in range(3):
        wide[d, 0:size] = jnp.broadcast_to(sbuf[pl.ds(start, size), d : d + 1], (size, LANES))


def cubes(wide, q_ref, start, size):
    his, los = [], []
    for j in range(CHUNK // LANES):
        at = pl.ds(pl.multiple_of(start + j * LANES, LANES), LANES)
        dx = wide[0, 0:size] - q_ref[0:1, at]
        dy = wide[1, 0:size] - q_ref[1:2, at]
        dz = wide[2, 0:size] - q_ref[2:3, at]
        inverse = lax.rsqrt((dx * dx + CORE) + (dy * dy + dz * dz))
        hi, lo = split(inverse * inverse * inverse)
        his.append(hi)
        los.append(lo)
    return jnp.concatenate(his, axis=1), jnp.concatenate(los, axis=1)


def traction_kernel(scale, groups_ref, q_ref, kq_ref, out_ref, sent_ref, kept_ref, sbuf, wide, total):
    q_dev = q_ref.shape[1]
    _, length, _ = assemble(groups_ref, sbuf)
    total[...] = jnp.zeros_like(total)

    def chunk(start, size):
        spread(sbuf, wide, start, size)
        vectors = jnp.concatenate(split(sbuf[pl.ds(start, size), 0:ROWS].T), axis=0)
        vectors = jnp.concatenate([vectors, vectors], axis=1)
        slot = jnp.minimum(start // CHUNK, KEPT)

        def block(j, c):
            at = pl.multiple_of(j * CHUNK, CHUNK)
            hi, lo = cubes(wide, q_ref, at, size)
            kept_ref[slot, 0, 0:size, pl.ds(at, CHUNK)] = hi
            kept_ref[slot, 1, 0:size, pl.ds(at, CHUNK)] = lo
            weights = jnp.concatenate([hi, lo], axis=0)
            total[:, pl.ds(at, CHUNK)] += jnp.dot(vectors, weights, preferred_element_type=F32)
            return c

        lax.fori_loop(0, q_dev // CHUNK, block, jnp.int32(0), unroll=8)

    in_chunks(length, chunk)
    both = (total[0:ROWS, :] + total[ROWS : 2 * ROWS, :]) * scale
    out_ref[...] = jnp.zeros_like(out_ref)
    out_ref[0:3, :] = both[3:6, :]
    half = q_dev // 2
    for p in range(2):
        at = slice(p * half, (p + 1) * half)
        sent_ref[4 * p : 4 * p + 3, :] = both[3:6, at]
        sent_ref[4 * p + 3 : 4 * p + 4, :] = kq_ref[0:1, at]


def nodes_of(nodes_ref, r, n):
    return nodes_ref[pl.ds(pl.multiple_of(r * n, n), n), :]


def set_hot(nodes, out_ref, first):
    rows = out_ref.shape[0]
    for k in range(nodes.shape[0]):
        row = nodes[k : k + 1, :] // LANES - first
        here = jnp.where(iota((rows, LANES), 0) == row, 1.0, 0.0)
        out_ref[:, k * LANES : (k + 1) * LANES] = here.astype(BF16)


def set_spot(nodes, out_ref):
    for k in range(nodes.shape[0]):
        here = jnp.where(iota((LANES, LANES), 0) == nodes[k : k + 1, :] % LANES, 1.0, 0.0)
        out_ref[:, k * LANES : (k + 1) * LANES] = here.astype(BF16)


def spread_points(spot_ref, values, cols):
    n = spot_ref.shape[1]
    for p, parts in enumerate(split(values)):
        for c in range(3):
            to = (p * 3 + c) * LANES
            for k in range(0, n, CHUNK):
                at = slice(k, k + CHUNK)
                part = jnp.broadcast_to(parts[c : c + 1, at], (LANES, CHUNK))
                cols[to : to + LANES, at] = spot_ref[:, at] * part


def layers(hot, cols):
    out = lax.dot_general(hot, cols, NT, preferred_element_type=F32)
    half = 3 * LANES
    return out[:, :half] + out[:, half:]


def set_parts(parts, place, x, rows, tile):
    hi, lo = split(tile)
    to = slice(place * LANES, (place + 1) * LANES)
    parts[to, x * LANES : (x + 1) * LANES] = hi
    parts[to, rows + x * LANES : rows + (x + 1) * LANES] = lo


def pair(nodes, k):
    return jnp.concatenate([nodes[k : k + 1, :], nodes[k + 1 : k + 2, :]], axis=1)


def gather(nodes, hot_ref, parts, fields, out_ref, first):
    for k in range(0, nodes.shape[0], 2):
        at = slice(k * LANES, (k + 2) * LANES)
        here = hot_ref[0 : parts.shape[1] // 2, at]
        found = jnp.dot(parts[...], jnp.concatenate([here, here], axis=0), preferred_element_type=F32)
        pick = iota((LANES, 2 * LANES), 0) == pair(nodes, k) % LANES
        for f in range(fields):
            value = jnp.where(pick, found[f * LANES : (f + 1) * LANES, :], 0.0)
            out_ref[first + f : first + f + 1, at] = jnp.sum(value, axis=0, keepdims=True)


def prepare_kernel(where_ref, nodes_ref, k_ref, kq_ref, kz_ref, hot_ref, parts):
    rows = k_ref.shape[0]
    n = kq_ref.shape[1] // LANES
    nodes = nodes_of(nodes_ref, where_ref[0], n)
    set_hot(nodes, hot_ref.at[0:rows], 0)
    set_spot(nodes, hot_ref.at[rows : rows + LANES])
    kz_ref[...] = jnp.zeros_like(kz_ref)
    for x in range(rows // LANES):
        at = slice(x * LANES, (x + 1) * LANES)
        tile = k_ref[at, :].T
        kz_ref[0:1, at] = tile[0:1, :]
        set_parts(parts, 0, x, rows, tile)
    kq_ref[...] = jnp.zeros_like(kq_ref)
    gather(nodes, hot_ref, parts, 1, kq_ref, 0)


def scatter_kernel(
    where_ref, nodes_ref, t_ref, hot_ref, b_ref, g_ref, low_ref, next_ref, high_ref, cols, parts
):
    n = t_ref.shape[1] // LANES
    rows = b_ref.shape[1]
    spread_points(hot_ref.at[rows : rows + LANES], t_ref[...], cols)
    load = layers(hot_ref[0:rows, :], cols[...])
    for ref in (low_ref, next_ref, high_ref):
        ref[...] = jnp.zeros_like(ref)
    for c in range(3):
        for x in range(rows // LANES):
            at = slice(x * LANES, (x + 1) * LANES)
            f = load[at, c * LANES : (c + 1) * LANES]
            b_ref[c, at, :] = f
            tile = f.T
            set_parts(parts, c, x, rows, tile)
            low_ref[c : c + 1, at] = tile[0:1, :]
            next_ref[c : c + 1, at] = tile[1:2, :]
            high_ref[c : c + 1, at] = tile[LANES - 1 : LANES, :]
    g_ref[...] = jnp.zeros_like(g_ref)
    gather(nodes_of(nodes_ref, where_ref[0], n), hot_ref, parts, 3, g_ref, 0)


def unfold(sent):
    return jnp.concatenate([sent[0:4], sent[4:8]], axis=1)


def sides_kernel(
    n_seg, where_ref, nodes_ref, left_ref, right_ref, low_ref, next_ref, high_ref, kz_ref,
    sides_ref, down_ref, up_ref, hot, spot, cols,
):
    n = hot.shape[1] // LANES
    rows = low_ref.shape[1]
    me = where_ref[0]
    down_ref[...] = jnp.zeros_like(down_ref)
    up_ref[...] = jnp.zeros_like(up_ref)
    own = slice(LANES, LANES + rows)
    down_ref[0:3, own] = low_ref[0:3, :]
    down_ref[3:6, own] = next_ref[0:3, :]
    down_ref[6:7, own] = kz_ref[0:1, :]
    up_ref[0:3, own] = high_ref[0:3, :]

    nodes = nodes_of(nodes_ref, jnp.maximum(me - 1, 0), n)
    set_hot(nodes, hot.at[0:LANES], rows - LANES)
    set_spot(nodes, spot)
    spread_points(spot, unfold(left_ref[...]) * jnp.where(me > 0, 1.0, 0.0), cols)
    left = layers(hot[0:LANES, :], cols[...])
    nodes = nodes_of(nodes_ref, jnp.minimum(me + 1, n_seg - 1), n)
    set_hot(nodes, hot, 0)
    set_spot(nodes, spot)
    t = unfold(right_ref[...])
    kq = t[3:4]
    t = t * jnp.where(me < n_seg - 1, 1.0, 0.0)
    spread_points(spot, t, cols)
    right = layers(hot[...], cols[...])
    spread_points(spot, t * kq, cols)
    stiff = layers(hot[0:LANES, :], cols[...])
    last = slice(LANES + rows, 2 * LANES + rows)
    for c in range(3):
        comp = slice(c * LANES, (c + 1) * LANES)
        sides_ref[c] = left[:, comp]
        sides_ref[3 + c] = right[0:LANES, comp]
        sides_ref[6 + c] = right[LANES : 2 * LANES, comp]
        sides_ref[9 + c] = stiff[:, comp]
        down_ref[c : c + 1, 0:LANES] = left[:, comp].T[0:1, :]
        tile = right[0:LANES, comp].T
        down_ref[c : c + 1, last] = tile[0:1, :]
        up_ref[c : c + 1, last] = tile[LANES - 1 : LANES, :]


def before_in_layer(f):
    i, j = iota(f.shape, 0), iota(f.shape, 1)
    return jnp.where(i == 0, 0.0, pltpu.roll(f, 1, 0)) + jnp.where(j == 0, 0.0, pltpu.roll(f, 1, 1))


def beside_in_layer(f):
    i, j = iota(f.shape, 0), iota(f.shape, 1)
    n, m = f.shape
    up = jnp.where(i == 0, 0.0, pltpu.roll(f, 1, 0)) + jnp.where(i == n - 1, 0.0, pltpu.roll(f, n - 1, 0))
    return up + (jnp.where(j == 0, 0.0, pltpu.roll(f, 1, 1)) + jnp.where(j == m - 1, 0.0, pltpu.roll(f, m - 1, 1)))


def operate_kernel(
    where_ref, nodes_ref, b_ref, sides_ref, k_ref, g_ref, hot_ref, u_ref, ur_ref, motion_ref, high_ref, parts
):
    n = g_ref.shape[1] // LANES
    rows = b_ref.shape[1]
    wide = rows // LANES
    high_ref[...] = jnp.zeros_like(high_ref)
    for c in range(3):
        b4 = sides_ref[3 + c]
        field = [sides_ref[c]] + [b_ref[c, x * LANES : (x + 1) * LANES, :] for x in range(wide)] + [b4]
        for x in range(wide):
            at = slice(x * LANES, (x + 1) * LANES)
            f = field[x + 1]
            u = (6.0 + k_ref[at, :]) * f - (beside_in_layer(f) + (field[x] + field[x + 2]))
            u_ref[c, at, :] = u
            tile = u.T
            high_ref[c : c + 1, at] = tile[LANES - 1 : LANES, :]
            set_parts(parts, c, x, rows, tile)
        ur_ref[c] = 6.0 * b4 + sides_ref[9 + c] - (field[wide] + sides_ref[6 + c] + beside_in_layer(b4))
    motion_ref[...] = g_ref[...]
    gather(nodes_of(nodes_ref, where_ref[0], n), hot_ref, parts, 3, motion_ref, 3)


def ends_kernel(
    n_seg, n_fe, where_ref, nodes_ref, b_ref, u_ref, ur_ref, k_ref, above_ref, below_ref, uh_ref, high_ref, g_ref,
    hot_ref, out_ref, motion_ref, sums_ref,
):
    n = g_ref.shape[1] // LANES
    rows = b_ref.shape[1]
    wide = rows // LANES
    me, block = where_ref[0], where_ref[1]
    is_above = jnp.where(block < n_fe - 1, 1.0, 0.0)
    above = above_ref[...] * is_above
    below = below_ref[...] * jnp.where(block > 0, 1.0, 0.0)
    own = slice(LANES, LANES + rows)

    center = above[0:3, own]
    place = iota(center.shape, 1) % LANES
    beside = above[0:3, 0:rows] + above[0:3, 2 * LANES : 2 * LANES + rows]
    beside = beside + jnp.where(place == 0, 0.0, pltpu.roll(center, 1, 1))
    beside = beside + jnp.where(place == LANES - 1, 0.0, pltpu.roll(center, rows - 1, 1))
    beside = beside + high_ref[0:3, :] + above[3:6, own]
    next_u = (6.0 + above[6:7, own]) * center - beside
    crossing = is_above * jnp.sum((uh_ref[0:3, :] - center) * next_u)

    above_t, below_t = above.T, below.T
    lane = iota((LANES, LANES), 1)
    zero = jnp.zeros((LANES, LANES), F32)
    bb, bu, uu, uau = zero, zero, zero, zero
    not_last = jnp.where(me < n_seg - 1, 1.0, 0.0)

    def ends(c, x):
        at = slice((x + 1) * LANES, (x + 2) * LANES)
        low = jnp.where(lane == 0, below_t[at, c : c + 1], 0.0)
        return low + jnp.where(lane == LANES - 1, above_t[at, c : c + 1], 0.0)

    for c in range(3):
        us = []
        for x in range(wide):
            at = slice(x * LANES, (x + 1) * LANES)
            f = b_ref[c, at, :]
            u = u_ref[c, at, :] - ends(c, x)
            out_ref[c, at, :] = u
            us.append(u)
            bb = bb + f * f
            bu = bu + f * u
            uu = uu + u * u
        us.append(not_last * (ur_ref[c] - ends(c, wide)))
        for x in range(wide):
            at = slice(x * LANES, (x + 1) * LANES)
            beside = before_in_layer(us[x]) + us[x + 1]
            uau = uau + us[x] * ((6.0 + k_ref[at, :]) * us[x] - 2.0 * beside)
    line = iota((1, LANES), 1)
    sums = jnp.where(line == 3, -2.0 * crossing, 0.0)
    for i, part in enumerate((bb, bu, uu, uau)):
        sums = sums + jnp.where(line == i, jnp.sum(part), 0.0)
    sums_ref[...] = jnp.broadcast_to(sums, sums_ref.shape)

    nodes = nodes_of(nodes_ref, me, n)
    faces = jnp.concatenate(split(below[:, own]) + split(above[:, own]), axis=0)
    motion_ref[...] = g_ref[...]
    for k in range(0, n, 2):
        at = slice(k * LANES, (k + 2) * LANES)
        found = jnp.dot(faces, hot_ref[0:rows, at], preferred_element_type=F32)
        last = pair(nodes, k) % LANES
        extra = jnp.where(last == 0, found[0:3] + found[8:11], 0.0)
        extra = extra + jnp.where(last == LANES - 1, found[16:19] + found[24:27], 0.0)
        motion_ref[3:6, at] = g_ref[3:6, at] - extra


def stress_kernel(groups_ref, kept_ref, q_ref, g_ref, sums_ref, out_ref, sbuf, wide, results, motion):
    q_dev = q_ref.shape[1]
    n_groups, _, width = out_ref.shape
    places, length, longest = measured(groups_ref)
    motion[...] = jnp.concatenate(split(g_ref[...]), axis=0)
    n_chunks = (length + (CHUNK - 1)) // CHUNK

    def from_kept(start, size):
        i = start // CHUNK
        m = motion[...]
        found = lax.dot_general(kept_ref[i, 0, 0:size], m, NT, preferred_element_type=F32)
        found = found + lax.dot_general(kept_ref[i, 1, 0:size], m, NT, preferred_element_type=F32)
        results[pl.ds(start, size), 0 : 2 * ROWS] = found

    in_chunks(jnp.minimum(length, KEPT * CHUNK), from_kept)

    def again(i, carry):
        start = pl.multiple_of(i * CHUNK, CHUNK)
        spread(sbuf, wide, start, CHUNK)

        def block(j, total):
            at = pl.multiple_of(j * CHUNK, CHUNK)
            hi, lo = cubes(wide, q_ref, at, CHUNK)
            m = motion[:, pl.ds(at, CHUNK)]
            total = total + lax.dot_general(hi, m, NT, preferred_element_type=F32)
            return total + lax.dot_general(lo, m, NT, preferred_element_type=F32)

        results[pl.ds(start, CHUNK), 0 : 2 * ROWS] = lax.fori_loop(
            0, q_dev // CHUNK, block, jnp.zeros((CHUNK, 2 * ROWS), F32), unroll=8
        )
        return carry

    @pl.when(n_chunks > KEPT)
    def _():
        assemble(groups_ref, sbuf)
        lax.fori_loop(KEPT, n_chunks, again, jnp.int32(0))

    def run(rows):
        row = iota((ROWS, rows), 0)
        for r, (offset, count) in enumerate(places):
            found = results[pl.ds(offset, rows), 0 : 2 * ROWS].T
            found = found[0:ROWS] + found[ROWS : 2 * ROWS]
            found = jnp.where(iota((ROWS, rows), 1) < count, found, 0.0)
            out_ref[r, :, 0:rows] = jnp.where(row == 6, sums_ref[:, 0:rows], found)
            if rows < width:
                out_ref[r, :, rows:width] = jnp.zeros((ROWS, width - rows), F32)

    by_width(longest, width, run)


def unpack_kernel(where_ref, tile_ref, partial_ref, out_ref):
    _, place = near_rank(tile_ref[...], where_ref[1])
    total = jnp.sum(partial_ref[...], axis=0)
    spreaded = jnp.dot(total, place, precision=HIGH, preferred_element_type=F32)
    total = jnp.where(iota(total.shape, 0) == 6, total, spreaded)
    out_ref[...] = jnp.broadcast_to(total[None], out_ref.shape)


def finish_kernel(scale, partial_ref, b_ref, u_ref, correction_ref, stress_ref):
    total = jnp.sum(partial_ref[...], axis=0)
    bb, bu, uu, uau = [total[6:7, i : i + 1] for i in range(4)]
    alpha = bb / bu
    later = bb - 2.0 * alpha * bu + alpha * alpha * uu
    beta = later / bb
    grow = 1.0 + beta
    alpha_next = later / (grow * grow * bu - 2.0 * alpha * grow * uu + alpha * alpha * uau)
    on_b = alpha + alpha_next * grow
    on_u = -alpha_next * alpha
    stress_ref[...] = (on_b * total[0:3] + on_u * total[3:6]) * scale
    for c in range(3):
        correction_ref[c] = on_b * b_ref[c] + on_u * u_ref[c]


def call(kernel, out, scratch=(), smem=0, inputs=0, flops=0, moved=0, limit=VMEM_LIMIT):
    vmem = pl.BlockSpec(memory_space=pltpu.VMEM)
    ints = pl.BlockSpec(memory_space=pltpu.SMEM)
    shapes = []
    for o in out:
        shapes.append(o if isinstance(o, jax.ShapeDtypeStruct) else jax.ShapeDtypeStruct(o, F32))
    single = len(shapes) == 1
    return pl.pallas_call(
        kernel,
        out_shape=shapes[0] if single else tuple(shapes),
        in_specs=[ints] * smem + [vmem] * inputs,
        out_specs=vmem if single else (vmem,) * len(shapes),
        scratch_shapes=list(scratch),
        compiler_params=pltpu.CompilerParams(vmem_limit_bytes=limit),
        cost_estimate=pl.CostEstimate(flops=flops, bytes_accessed=moved, transcendentals=0),
    )


def shards(seg_pos, burgers, seg_tile, quad_pos, quad_node, stiffness):
    n_seg, n_fe = lax.axis_size("seg"), lax.axis_size("fe")
    column, block = lax.axis_index("seg"), lax.axis_index("fe")
    s_dev = seg_pos.shape[1]
    q_block = quad_pos.shape[1]
    q_dev = q_block // n_seg
    total_segs = s_dev * n_seg
    total_points = q_block * n_fe
    wide, tall, deep = stiffness.shape
    rows = wide * tall
    where = jnp.stack([column, block]).astype(jnp.int32)
    tile = seg_tile.reshape(1, s_dev)
    nodes = quad_node.reshape(q_block // LANES, LANES)
    points = lax.dynamic_slice_in_dim(quad_pos, column * q_dev, q_dev, 1)
    stiff = stiffness.reshape(rows, deep)

    up_seg = [(i, (i + 1) % n_seg) for i in range(n_seg)]
    down_seg = [((i + 1) % n_seg, i) for i in range(n_seg)]
    up_fe = [(i, (i + 1) % n_fe) for i in range(n_fe)]
    down_fe = [((i + 1) % n_fe, i) for i in range(n_fe)]
    field, line = (3, rows, deep), (ROWS, q_dev)
    face, message = (ROWS, rows), (ROWS, rows + 2 * LANES)
    long = total_segs + 2 * CHUNK
    sbuf = pltpu.VMEM((long, LANES), F32)
    spreaded = pltpu.VMEM((3, CHUNK, LANES), F32)
    cols = pltpu.VMEM((6 * LANES, q_dev), BF16)

    packed = call(
        pack_kernel, [(n_seg, ROWS, s_dev)], smem=1, inputs=3, limit=PACK_LIMIT
    )(where, seg_pos, burgers, tile)
    groups = lax.all_to_all(packed, "seg", 0, 0, tiled=True)
    kq, kz, hot = call(
        prepare_kernel, [line, face, jax.ShapeDtypeStruct((rows + LANES, q_dev), BF16)],
        [pltpu.VMEM((LANES, 2 * rows), BF16)], smem=1, inputs=2, flops=10**9, moved=10**6, limit=PACK_LIMIT,
    )(where, nodes, stiff)

    def traction(*refs):
        traction_kernel(STRENGTH / math.sqrt(total_segs), *refs)

    weights = jax.ShapeDtypeStruct((KEPT + 1, 2, CHUNK, q_dev), BF16)
    t, sent, kept = call(
        traction, [line, (ROWS, q_dev // 2), weights], [sbuf, spreaded, pltpu.VMEM((2 * ROWS, q_dev), F32)], inputs=3,
        flops=10**10, moved=10**6,
    )(groups, points, kq[0:1])
    from_left = lax.ppermute(sent, "seg", up_seg)
    from_right = lax.ppermute(sent, "seg", down_seg)

    b, g, low, after, high = call(
        scatter_kernel, [field, line, face, face, face], [cols, pltpu.VMEM((3 * LANES, 2 * rows), BF16)],
        smem=1, inputs=3, flops=4 * 10**9, moved=4 * 10**6,
    )(where, nodes, t, hot)

    def fill_sides(*refs):
        sides_kernel(n_seg, *refs)

    sides, down, up = call(
        fill_sides, [(12, tall, deep), message, message],
        [pltpu.VMEM((2 * LANES, q_dev), BF16), pltpu.VMEM((LANES, q_dev), BF16), cols],
        smem=1, inputs=7, flops=2 * 10**9, moved=10**6,
    )(where, nodes, from_left, from_right, low, after, high, kz)
    above = lax.ppermute(down, "fe", down_fe)
    below = lax.ppermute(up, "fe", up_fe)
    u, ur, g, uh = call(
        operate_kernel, [field, (3, tall, deep), line, face], [pltpu.VMEM((3 * LANES, 2 * rows), BF16)],
        smem=1, inputs=6, flops=4 * 10**9, moved=4 * 10**6,
    )(where, nodes, b, sides, stiff, g, hot)

    def fill_ends(*refs):
        ends_kernel(n_seg, n_fe, *refs)

    u, motion, sums = call(
        fill_ends, [field, line, (ROWS, LANES)], smem=1, inputs=11, flops=10**9, moved=4 * 10**6
    )(where, nodes, b, u, ur, stiff, above, below, uh, high, g, hot)
    partial = call(
        stress_kernel, [(n_seg, ROWS, s_dev)],
        [sbuf, spreaded, pltpu.VMEM((long, LANES), F32), pltpu.VMEM((2 * ROWS, q_dev), BF16)],
        inputs=5, flops=10**10, moved=10**6,
    )(groups, kept, points, motion, sums)
    partial = lax.all_to_all(partial, "seg", 0, 0, tiled=True)
    partial = call(unpack_kernel, [(n_fe, ROWS, s_dev)], smem=1, inputs=2)(where, tile, partial)
    partial = lax.all_to_all(partial, "fe", 0, 0, tiled=True)

    def finish(*refs):
        finish_kernel(4.0 * STRENGTH / math.sqrt(total_points), *refs)

    correction, stress = call(finish, [(3, rows, deep), (3, s_dev)], inputs=3)(partial, b, u)
    return correction.reshape(3, wide, tall, deep), stress


def solution(mesh):
    placed = (
        P(None, "seg"),
        P(None, "seg"),
        P("seg"),
        P(None, "fe"),
        P("fe"),
        P("seg", None, "fe"),
    )
    return jax.shard_map(
        shards,
        mesh=mesh,
        in_specs=placed,
        out_specs=(P(None, "seg", None, "fe"), P(None, "seg")),
        check_vma=False,
    )
```

```python
import math

import jax
import jax.numpy as jnp
from jax import lax
from jax.experimental import pallas as pl
from jax.experimental.pallas import tpu as pltpu
from jax.sharding import PartitionSpec as P

CORE = 0.0001
STRENGTH = 0.001
HIGH = lax.Precision.HIGHEST
F32 = jnp.float32
BF16 = jnp.bfloat16
ROWS = 8
LANES = 128
CHUNK = 256
KEPT = 7
NT = (((1,), (1,)), ((), ()))
VMEM_LIMIT = 12 * 1024 * 1024
PACK_LIMIT = 60 * 1024 * 1024


def iota(shape, dim):
    return lax.broadcasted_iota(jnp.int32, shape, dim)


def split(x):
    hi = x.astype(BF16)
    return hi, (x - hi.astype(F32)).astype(BF16)


def near_rank(tile, block):
    near = jnp.abs(tile - block) <= 1
    mask = jnp.where(near, 1.0, 0.0)
    n = tile.shape[1]
    before = jnp.where(iota((n, n), 0) < iota((n, n), 1), 1.0, 0.0)
    rank = jnp.dot(jnp.broadcast_to(mask, (ROWS, n)), before, preferred_element_type=F32)[:1]
    place = jnp.where(iota((n, n), 0) == rank.astype(jnp.int32), mask, 0.0)
    return mask, place


def pack_kernel(where_ref, pos_ref, burgers_ref, tile_ref, out_ref):
    mask, place = near_rank(tile_ref[...], where_ref[1])
    rest = jnp.broadcast_to(mask, (2, mask.shape[1]))
    segs = jnp.concatenate([pos_ref[...], burgers_ref[...], rest], axis=0)
    packed = lax.dot_general(segs, place, NT, precision=HIGH, preferred_element_type=F32)
    out_ref[...] = jnp.broadcast_to(packed[None], out_ref.shape)


def measured(groups_ref):
    offset, longest = 0, 0
    places = []
    for r in range(groups_ref.shape[0]):
        count = jnp.sum(groups_ref[r, 6:7, :]).astype(jnp.int32)
        places.append((offset, count))
        offset = offset + count
        longest = jnp.maximum(longest, count)
    return places, offset, longest


def by_width(longest, width, run):
    half = width // 2

    @pl.when(longest <= half)
    def _():
        run(half)

    @pl.when(longest > half)
    def _():
        run(width)


def assemble(groups_ref, sbuf):
    places, total, longest = measured(groups_ref)

    def run(rows):
        for r, (offset, _) in enumerate(places):
            sbuf[pl.ds(offset, rows), 0:ROWS] = groups_ref[r].T[0:rows]

    by_width(longest, groups_ref.shape[2], run)
    sbuf[pl.ds(total, CHUNK), 0:ROWS] = jnp.zeros((CHUNK, ROWS), F32)
    return places, total, longest


def in_chunks(total, chunk):
    quarter, half = CHUNK // 4, CHUNK // 2
    whole = total // CHUNK
    rest = total - whole * CHUNK
    n = whole + jnp.where(rest > half, 1, 0)

    def step(i, carry):
        chunk(pl.multiple_of(i * CHUNK, CHUNK), CHUNK)
        return carry

    lax.fori_loop(0, n, step, jnp.int32(0))
    for least, most in ((0, quarter), (quarter, half)):

        @pl.when(jnp.logical_and(rest > least, rest <= most))
        def _():
            chunk(pl.multiple_of(whole * CHUNK, CHUNK), most)


def spread(sbuf, wide, start, size):
    for d in range(3):
        wide[d, 0:size] = jnp.broadcast_to(sbuf[pl.ds(start, size), d : d + 1], (size, LANES))


def cubes(wide, q_ref, start, size):
    his, los = [], []
    for j in range(CHUNK // LANES):
        at = pl.ds(pl.multiple_of(start + j * LANES, LANES), LANES)
        dx = wide[0, 0:size] - q_ref[0:1, at]
        dy = wide[1, 0:size] - q_ref[1:2, at]
        dz = wide[2, 0:size] - q_ref[2:3, at]
        inverse = lax.rsqrt((dx * dx + CORE) + (dy * dy + dz * dz))
        hi, lo = split(inverse * inverse * inverse)
        his.append(hi)
        los.append(lo)
    return jnp.concatenate(his, axis=1), jnp.concatenate(los, axis=1)


def traction_kernel(scale, groups_ref, q_ref, kq_ref, out_ref, sent_ref, kept_ref, sbuf, wide, total):
    q_dev = q_ref.shape[1]
    _, length, _ = assemble(groups_ref, sbuf)
    total[...] = jnp.zeros_like(total)

    def chunk(start, size):
        spread(sbuf, wide, start, size)
        vectors = jnp.concatenate(split(sbuf[pl.ds(start, size), 0:ROWS].T), axis=0)
        vectors = jnp.concatenate([vectors, vectors], axis=1)
        slot = jnp.minimum(start // CHUNK, KEPT)

        def block(j, c):
            at = pl.multiple_of(j * CHUNK, CHUNK)
            hi, lo = cubes(wide, q_ref, at, size)
            kept_ref[slot, 0, 0:size, pl.ds(at, CHUNK)] = hi
            kept_ref[slot, 1, 0:size, pl.ds(at, CHUNK)] = lo
            weights = jnp.concatenate([hi, lo], axis=0)
            total[:, pl.ds(at, CHUNK)] += jnp.dot(vectors, weights, preferred_element_type=F32)
            return c

        lax.fori_loop(0, q_dev // CHUNK, block, jnp.int32(0), unroll=8)

    in_chunks(length, chunk)
    both = (total[0:ROWS, :] + total[ROWS : 2 * ROWS, :]) * scale
    out_ref[...] = jnp.zeros_like(out_ref)
    out_ref[0:3, :] = both[3:6, :]
    half = q_dev // 2
    for p in range(2):
        at = slice(p * half, (p + 1) * half)
        sent_ref[4 * p : 4 * p + 3, :] = both[3:6, at]
        sent_ref[4 * p + 3 : 4 * p + 4, :] = kq_ref[0:1, at]


def nodes_of(nodes_ref, r, n):
    return nodes_ref[pl.ds(pl.multiple_of(r * n, n), n), :]


def set_hot(nodes, out_ref, first):
    rows = out_ref.shape[0]
    for k in range(nodes.shape[0]):
        row = nodes[k : k + 1, :] // LANES - first
        here = jnp.where(iota((rows, LANES), 0) == row, 1.0, 0.0)
        out_ref[:, k * LANES : (k + 1) * LANES] = here.astype(BF16)


def set_spot(nodes, out_ref):
    for k in range(nodes.shape[0]):
        here = jnp.where(iota((LANES, LANES), 0) == nodes[k : k + 1, :] % LANES, 1.0, 0.0)
        out_ref[:, k * LANES : (k + 1) * LANES] = here.astype(BF16)


def spread_points(spot_ref, values, cols):
    n = spot_ref.shape[1]
    for p, parts in enumerate(split(values)):
        for c in range(3):
            to = (p * 3 + c) * LANES
            for k in range(0, n, CHUNK):
                at = slice(k, k + CHUNK)
                part = jnp.broadcast_to(parts[c : c + 1, at], (LANES, CHUNK))
                cols[to : to + LANES, at] = spot_ref[:, at] * part


def layers(hot, cols):
    out = lax.dot_general(hot, cols, NT, preferred_element_type=F32)
    half = 3 * LANES
    return out[:, :half] + out[:, half:]


def set_parts(parts, place, x, rows, tile):
    hi, lo = split(tile)
    to = slice(place * LANES, (place + 1) * LANES)
    parts[to, x * LANES : (x + 1) * LANES] = hi
    parts[to, rows + x * LANES : rows + (x + 1) * LANES] = lo


def pair(nodes, k):
    return jnp.concatenate([nodes[k : k + 1, :], nodes[k + 1 : k + 2, :]], axis=1)


def gather(nodes, hot_ref, parts, fields, out_ref, first):
    for k in range(0, nodes.shape[0], 2):
        at = slice(k * LANES, (k + 2) * LANES)
        here = hot_ref[0 : parts.shape[1] // 2, at]
        found = jnp.dot(parts[...], jnp.concatenate([here, here], axis=0), preferred_element_type=F32)
        pick = iota((LANES, 2 * LANES), 0) == pair(nodes, k) % LANES
        for f in range(fields):
            value = jnp.where(pick, found[f * LANES : (f + 1) * LANES, :], 0.0)
            out_ref[first + f : first + f + 1, at] = jnp.sum(value, axis=0, keepdims=True)


def prepare_kernel(where_ref, nodes_ref, k_ref, kq_ref, kz_ref, hot_ref, parts):
    rows = k_ref.shape[0]
    n = kq_ref.shape[1] // LANES
    nodes = nodes_of(nodes_ref, where_ref[0], n)
    set_hot(nodes, hot_ref.at[0:rows], 0)
    set_spot(nodes, hot_ref.at[rows : rows + LANES])
    kz_ref[...] = jnp.zeros_like(kz_ref)
    for x in range(rows // LANES):
        at = slice(x * LANES, (x + 1) * LANES)
        tile = k_ref[at, :].T
        kz_ref[0:1, at] = tile[0:1, :]
        set_parts(parts, 0, x, rows, tile)
    kq_ref[...] = jnp.zeros_like(kq_ref)
    gather(nodes, hot_ref, parts, 1, kq_ref, 0)


def scatter_kernel(
    where_ref, nodes_ref, t_ref, hot_ref, b_ref, g_ref, low_ref, next_ref, high_ref, cols, parts
):
    n = t_ref.shape[1] // LANES
    rows = b_ref.shape[1]
    spread_points(hot_ref.at[rows : rows + LANES], t_ref[...], cols)
    load = layers(hot_ref[0:rows, :], cols[...])
    for ref in (low_ref, next_ref, high_ref):
        ref[...] = jnp.zeros_like(ref)
    for c in range(3):
        for x in range(rows // LANES):
            at = slice(x * LANES, (x + 1) * LANES)
            f = load[at, c * LANES : (c + 1) * LANES]
            b_ref[c, at, :] = f
            tile = f.T
            set_parts(parts, c, x, rows, tile)
            low_ref[c : c + 1, at] = tile[0:1, :]
            next_ref[c : c + 1, at] = tile[1:2, :]
            high_ref[c : c + 1, at] = tile[LANES - 1 : LANES, :]
    g_ref[...] = jnp.zeros_like(g_ref)
    gather(nodes_of(nodes_ref, where_ref[0], n), hot_ref, parts, 3, g_ref, 0)


def unfold(sent):
    return jnp.concatenate([sent[0:4], sent[4:8]], axis=1)


def sides_kernel(
    n_seg, where_ref, nodes_ref, left_ref, right_ref, low_ref, next_ref, high_ref, kz_ref,
    sides_ref, down_ref, up_ref, hot, spot, cols,
):
    n = hot.shape[1] // LANES
    rows = low_ref.shape[1]
    me = where_ref[0]
    down_ref[...] = jnp.zeros_like(down_ref)
    up_ref[...] = jnp.zeros_like(up_ref)
    own = slice(LANES, LANES + rows)
    down_ref[0:3, own] = low_ref[0:3, :]
    down_ref[3:6, own] = next_ref[0:3, :]
    down_ref[6:7, own] = kz_ref[0:1, :]
    up_ref[0:3, own] = high_ref[0:3, :]

    nodes = nodes_of(nodes_ref, jnp.maximum(me - 1, 0), n)
    set_hot(nodes, hot.at[0:LANES], rows - LANES)
    set_spot(nodes, spot)
    spread_points(spot, unfold(left_ref[...]) * jnp.where(me > 0, 1.0, 0.0), cols)
    left = layers(hot[0:LANES, :], cols[...])
    nodes = nodes_of(nodes_ref, jnp.minimum(me + 1, n_seg - 1), n)
    set_hot(nodes, hot, 0)
    set_spot(nodes, spot)
    t = unfold(right_ref[...])
    kq = t[3:4]
    t = t * jnp.where(me < n_seg - 1, 1.0, 0.0)
    spread_points(spot, t, cols)
    right = layers(hot[...], cols[...])
    spread_points(spot, t * kq, cols)
    stiff = layers(hot[0:LANES, :], cols[...])
    last = slice(LANES + rows, 2 * LANES + rows)
    for c in range(3):
        comp = slice(c * LANES, (c + 1) * LANES)
        sides_ref[c] = left[:, comp]
        sides_ref[3 + c] = right[0:LANES, comp]
        sides_ref[6 + c] = right[LANES : 2 * LANES, comp]
        sides_ref[9 + c] = stiff[:, comp]
        down_ref[c : c + 1, 0:LANES] = left[:, comp].T[0:1, :]
        tile = right[0:LANES, comp].T
        down_ref[c : c + 1, last] = tile[0:1, :]
        up_ref[c : c + 1, last] = tile[LANES - 1 : LANES, :]


def before_in_layer(f):
    i, j = iota(f.shape, 0), iota(f.shape, 1)
    return jnp.where(i == 0, 0.0, pltpu.roll(f, 1, 0)) + jnp.where(j == 0, 0.0, pltpu.roll(f, 1, 1))


def beside_in_layer(f):
    i, j = iota(f.shape, 0), iota(f.shape, 1)
    n, m = f.shape
    up = jnp.where(i == 0, 0.0, pltpu.roll(f, 1, 0)) + jnp.where(i == n - 1, 0.0, pltpu.roll(f, n - 1, 0))
    return up + (jnp.where(j == 0, 0.0, pltpu.roll(f, 1, 1)) + jnp.where(j == m - 1, 0.0, pltpu.roll(f, m - 1, 1)))


def operate_kernel(
    where_ref, nodes_ref, b_ref, sides_ref, k_ref, g_ref, hot_ref, u_ref, ur_ref, motion_ref, high_ref, parts
):
    n = g_ref.shape[1] // LANES
    rows = b_ref.shape[1]
    wide = rows // LANES
    high_ref[...] = jnp.zeros_like(high_ref)
    for c in range(3):
        b4 = sides_ref[3 + c]
        field = [sides_ref[c]] + [b_ref[c, x * LANES : (x + 1) * LANES, :] for x in range(wide)] + [b4]
        for x in range(wide):
            at = slice(x * LANES, (x + 1) * LANES)
            f = field[x + 1]
            u = (6.0 + k_ref[at, :]) * f - (beside_in_layer(f) + (field[x] + field[x + 2]))
            u_ref[c, at, :] = u
            tile = u.T
            high_ref[c : c + 1, at] = tile[LANES - 1 : LANES, :]
            set_parts(parts, c, x, rows, tile)
        ur_ref[c] = 6.0 * b4 + sides_ref[9 + c] - (field[wide] + sides_ref[6 + c] + beside_in_layer(b4))
    motion_ref[...] = g_ref[...]
    gather(nodes_of(nodes_ref, where_ref[0], n), hot_ref, parts, 3, motion_ref, 3)


def ends_kernel(
    n_seg, n_fe, where_ref, nodes_ref, b_ref, u_ref, ur_ref, k_ref, above_ref, below_ref, uh_ref, high_ref, g_ref,
    hot_ref, out_ref, motion_ref, sums_ref,
):
    n = g_ref.shape[1] // LANES
    rows = b_ref.shape[1]
    wide = rows // LANES
    me, block = where_ref[0], where_ref[1]
    is_above = jnp.where(block < n_fe - 1, 1.0, 0.0)
    above = above_ref[...] * is_above
    below = below_ref[...] * jnp.where(block > 0, 1.0, 0.0)
    own = slice(LANES, LANES + rows)

    center = above[0:3, own]
    place = iota(center.shape, 1) % LANES
    beside = above[0:3, 0:rows] + above[0:3, 2 * LANES : 2 * LANES + rows]
    beside = beside + jnp.where(place == 0, 0.0, pltpu.roll(center, 1, 1))
    beside = beside + jnp.where(place == LANES - 1, 0.0, pltpu.roll(center, rows - 1, 1))
    beside = beside + high_ref[0:3, :] + above[3:6, own]
    next_u = (6.0 + above[6:7, own]) * center - beside
    crossing = is_above * jnp.sum((uh_ref[0:3, :] - center) * next_u)

    above_t, below_t = above.T, below.T
    lane = iota((LANES, LANES), 1)
    zero = jnp.zeros((LANES, LANES), F32)
    bb, bu, uu, uau = zero, zero, zero, zero
    not_last = jnp.where(me < n_seg - 1, 1.0, 0.0)

    def ends(c, x):
        at = slice((x + 1) * LANES, (x + 2) * LANES)
        low = jnp.where(lane == 0, below_t[at, c : c + 1], 0.0)
        return low + jnp.where(lane == LANES - 1, above_t[at, c : c + 1], 0.0)

    for c in range(3):
        us = []
        for x in range(wide):
            at = slice(x * LANES, (x + 1) * LANES)
            f = b_ref[c, at, :]
            u = u_ref[c, at, :] - ends(c, x)
            out_ref[c, at, :] = u
            us.append(u)
            bb = bb + f * f
            bu = bu + f * u
            uu = uu + u * u
        us.append(not_last * (ur_ref[c] - ends(c, wide)))
        for x in range(wide):
            at = slice(x * LANES, (x + 1) * LANES)
            beside = before_in_layer(us[x]) + us[x + 1]
            uau = uau + us[x] * ((6.0 + k_ref[at, :]) * us[x] - 2.0 * beside)
    line = iota((1, LANES), 1)
    sums = jnp.where(line == 3, -2.0 * crossing, 0.0)
    for i, part in enumerate((bb, bu, uu, uau)):
        sums = sums + jnp.where(line == i, jnp.sum(part), 0.0)
    sums_ref[...] = jnp.broadcast_to(sums, sums_ref.shape)

    nodes = nodes_of(nodes_ref, me, n)
    faces = jnp.concatenate(split(below[:, own]) + split(above[:, own]), axis=0)
    motion_ref[...] = g_ref[...]
    for k in range(0, n, 2):
        at = slice(k * LANES, (k + 2) * LANES)
        found = jnp.dot(faces, hot_ref[0:rows, at], preferred_element_type=F32)
        last = pair(nodes, k) % LANES
        extra = jnp.where(last == 0, found[0:3] + found[8:11], 0.0)
        extra = extra + jnp.where(last == LANES - 1, found[16:19] + found[24:27], 0.0)
        motion_ref[3:6, at] = g_ref[3:6, at] - extra


def stress_kernel(groups_ref, kept_ref, q_ref, g_ref, sums_ref, out_ref, sbuf, wide, results, motion):
    q_dev = q_ref.shape[1]
    n_groups, _, width = out_ref.shape
    places, length, longest = measured(groups_ref)
    motion[...] = jnp.concatenate(split(g_ref[...]), axis=0)
    n_chunks = (length + (CHUNK - 1)) // CHUNK

    def from_kept(start, size):
        i = start // CHUNK
        m = motion[...]
        found = lax.dot_general(kept_ref[i, 0, 0:size], m, NT, preferred_element_type=F32)
        found = found + lax.dot_general(kept_ref[i, 1, 0:size], m, NT, preferred_element_type=F32)
        results[pl.ds(start, size), 0 : 2 * ROWS] = found

    in_chunks(jnp.minimum(length, KEPT * CHUNK), from_kept)

    def again(i, carry):
        start = pl.multiple_of(i * CHUNK, CHUNK)
        spread(sbuf, wide, start, CHUNK)

        def block(j, total):
            at = pl.multiple_of(j * CHUNK, CHUNK)
            hi, lo = cubes(wide, q_ref, at, CHUNK)
            m = motion[:, pl.ds(at, CHUNK)]
            total = total + lax.dot_general(hi, m, NT, preferred_element_type=F32)
            return total + lax.dot_general(lo, m, NT, preferred_element_type=F32)

        results[pl.ds(start, CHUNK), 0 : 2 * ROWS] = lax.fori_loop(
            0, q_dev // CHUNK, block, jnp.zeros((CHUNK, 2 * ROWS), F32), unroll=8
        )
        return carry

    @pl.when(n_chunks > KEPT)
    def _():
        assemble(groups_ref, sbuf)
        lax.fori_loop(KEPT, n_chunks, again, jnp.int32(0))

    def run(rows):
        row = iota((ROWS, rows), 0)
        for r, (offset, count) in enumerate(places):
            found = results[pl.ds(offset, rows), 0 : 2 * ROWS].T
            found = found[0:ROWS] + found[ROWS : 2 * ROWS]
            found = jnp.where(iota((ROWS, rows), 1) < count, found, 0.0)
            out_ref[r, :, 0:rows] = jnp.where(row == 6, sums_ref[:, 0:rows], found)
            if rows < width:
                out_ref[r, :, rows:width] = jnp.zeros((ROWS, width - rows), F32)

    by_width(longest, width, run)


def unpack_kernel(where_ref, tile_ref, partial_ref, out_ref):
    _, place = near_rank(tile_ref[...], where_ref[1])
    total = jnp.sum(partial_ref[...], axis=0)
    spreaded = jnp.dot(total, place, precision=HIGH, preferred_element_type=F32)
    total = jnp.where(iota(total.shape, 0) == 6, total, spreaded)
    out_ref[...] = jnp.broadcast_to(total[None], out_ref.shape)


def finish_kernel(scale, partial_ref, b_ref, u_ref, correction_ref, stress_ref):
    total = jnp.sum(partial_ref[...], axis=0)
    bb, bu, uu, uau = [total[6:7, i : i + 1] for i in range(4)]
    alpha = bb / bu
    later = bb - 2.0 * alpha * bu + alpha * alpha * uu
    beta = later / bb
    grow = 1.0 + beta
    alpha_next = later / (grow * grow * bu - 2.0 * alpha * grow * uu + alpha * alpha * uau)
    on_b = alpha + alpha_next * grow
    on_u = -alpha_next * alpha
    stress_ref[...] = (on_b * total[0:3] + on_u * total[3:6]) * scale
    for c in range(3):
        correction_ref[c] = on_b * b_ref[c] + on_u * u_ref[c]


def call(kernel, out, scratch=(), placed=False, inputs=0, flops=0, moved=0, limit=VMEM_LIMIT):
    vmem = pl.BlockSpec(memory_space=pltpu.VMEM)
    shapes = []
    for o in out:
        shapes.append(o if isinstance(o, jax.ShapeDtypeStruct) else jax.ShapeDtypeStruct(o, F32))
    single = len(shapes) == 1

    def with_place(*refs):
        kernel((lax.axis_index("seg"), lax.axis_index("fe")), *refs)

    return pl.pallas_call(
        with_place if placed else kernel,
        out_shape=shapes[0] if single else tuple(shapes),
        in_specs=[vmem] * inputs,
        out_specs=vmem if single else (vmem,) * len(shapes),
        scratch_shapes=list(scratch),
        compiler_params=pltpu.CompilerParams(vmem_limit_bytes=limit),
        cost_estimate=pl.CostEstimate(flops=flops, bytes_accessed=moved, transcendentals=0),
    )


def shards(seg_pos, burgers, seg_tile, quad_pos, quad_node, stiffness):
    n_seg, n_fe = lax.axis_size("seg"), lax.axis_size("fe")
    column = lax.axis_index("seg")
    s_dev = seg_pos.shape[1]
    q_block = quad_pos.shape[1]
    q_dev = q_block // n_seg
    total_segs = s_dev * n_seg
    total_points = q_block * n_fe
    wide, tall, deep = stiffness.shape
    rows = wide * tall
    tile = seg_tile.reshape(1, s_dev)
    nodes = quad_node.reshape(q_block // LANES, LANES)
    points = lax.dynamic_slice_in_dim(quad_pos, column * q_dev, q_dev, 1)
    stiff = stiffness.reshape(rows, deep)

    up_seg = [(i, (i + 1) % n_seg) for i in range(n_seg)]
    down_seg = [((i + 1) % n_seg, i) for i in range(n_seg)]
    up_fe = [(i, (i + 1) % n_fe) for i in range(n_fe)]
    down_fe = [((i + 1) % n_fe, i) for i in range(n_fe)]
    field, line = (3, rows, deep), (ROWS, q_dev)
    face, message = (ROWS, rows), (ROWS, rows + 2 * LANES)
    long = total_segs + 2 * CHUNK
    sbuf = pltpu.VMEM((long, LANES), F32)
    spreaded = pltpu.VMEM((3, CHUNK, LANES), F32)
    cols = pltpu.VMEM((6 * LANES, q_dev), BF16)

    packed = call(
        pack_kernel, [(n_seg, ROWS, s_dev)], placed=True, inputs=3, limit=PACK_LIMIT
    )(seg_pos, burgers, tile)
    groups = lax.all_to_all(packed, "seg", 0, 0, tiled=True)
    kq, kz, hot = call(
        prepare_kernel, [line, face, jax.ShapeDtypeStruct((rows + LANES, q_dev), BF16)],
        [pltpu.VMEM((LANES, 2 * rows), BF16)], placed=True, inputs=2, flops=10**9, moved=10**6, limit=PACK_LIMIT,
    )(nodes, stiff)

    def traction(*refs):
        traction_kernel(STRENGTH / math.sqrt(total_segs), *refs)

    weights = jax.ShapeDtypeStruct((KEPT + 1, 2, CHUNK, q_dev), BF16)
    t, sent, kept = call(
        traction, [line, (ROWS, q_dev // 2), weights], [sbuf, spreaded, pltpu.VMEM((2 * ROWS, q_dev), F32)], inputs=3,
        flops=10**10, moved=10**6,
    )(groups, points, kq[0:1])
    from_left = lax.ppermute(sent, "seg", up_seg)
    from_right = lax.ppermute(sent, "seg", down_seg)

    b, g, low, after, high = call(
        scatter_kernel, [field, line, face, face, face], [cols, pltpu.VMEM((3 * LANES, 2 * rows), BF16)],
        placed=True, inputs=3, flops=4 * 10**9, moved=4 * 10**6,
    )(nodes, t, hot)

    def fill_sides(*refs):
        sides_kernel(n_seg, *refs)

    sides, down, up = call(
        fill_sides, [(12, tall, deep), message, message],
        [pltpu.VMEM((2 * LANES, q_dev), BF16), pltpu.VMEM((LANES, q_dev), BF16), cols],
        placed=True, inputs=7, flops=2 * 10**9, moved=10**6,
    )(nodes, from_left, from_right, low, after, high, kz)
    above = lax.ppermute(down, "fe", down_fe)
    below = lax.ppermute(up, "fe", up_fe)
    u, ur, g, uh = call(
        operate_kernel, [field, (3, tall, deep), line, face], [pltpu.VMEM((3 * LANES, 2 * rows), BF16)],
        placed=True, inputs=6, flops=4 * 10**9, moved=4 * 10**6,
    )(nodes, b, sides, stiff, g, hot)

    def fill_ends(*refs):
        ends_kernel(n_seg, n_fe, *refs)

    u, motion, sums = call(
        fill_ends, [field, line, (ROWS, LANES)], placed=True, inputs=11, flops=10**9, moved=4 * 10**6
    )(nodes, b, u, ur, stiff, above, below, uh, high, g, hot)
    partial = call(
        stress_kernel, [(n_seg, ROWS, s_dev)],
        [sbuf, spreaded, pltpu.VMEM((long, LANES), F32), pltpu.VMEM((2 * ROWS, q_dev), BF16)],
        inputs=5, flops=10**10, moved=10**6,
    )(groups, kept, points, motion, sums)
    partial = lax.all_to_all(partial, "seg", 0, 0, tiled=True)
    partial = call(unpack_kernel, [(n_fe, ROWS, s_dev)], placed=True, inputs=2)(tile, partial)
    partial = lax.all_to_all(partial, "fe", 0, 0, tiled=True)

    def finish(*refs):
        finish_kernel(4.0 * STRENGTH / math.sqrt(total_points), *refs)

    correction, stress = call(finish, [(3, rows, deep), (3, s_dev)], inputs=3)(partial, b, u)
    return correction.reshape(3, wide, tall, deep), stress


def solution(mesh):
    placed = (
        P(None, "seg"),
        P(None, "seg"),
        P("seg"),
        P(None, "fe"),
        P("fe"),
        P("seg", None, "fe"),
    )
    return jax.shard_map(
        shards,
        mesh=mesh,
        in_specs=placed,
        out_specs=(P(None, "seg", None, "fe"), P(None, "seg")),
        check_vma=False,
    )
```

```python
import math

import jax
import jax.numpy as jnp
from jax import lax
from jax.experimental import pallas as pl
from jax.experimental.pallas import tpu as pltpu
from jax.sharding import PartitionSpec as P

CORE = 0.0001
STRENGTH = 0.001
F32 = jnp.float32
BF16 = jnp.bfloat16
ROWS = 8
LANES = 128
CHUNK = 256
KEPT = 7
NT = (((1,), (1,)), ((), ()))
VMEM_LIMIT = 12 * 1024 * 1024
PACK_LIMIT = 60 * 1024 * 1024


def iota(shape, dim):
    return lax.broadcasted_iota(jnp.int32, shape, dim)


def split(x):
    hi = x.astype(BF16)
    return hi, (x - hi.astype(F32)).astype(BF16)


def thirds(x):
    high, rest = split(x)
    low = (x - high.astype(F32)) - rest.astype(F32)
    return jnp.concatenate([high, rest, low.astype(BF16)], axis=1)


def near_rank(tile, block):
    near = jnp.abs(tile - block) <= 1
    mask = jnp.where(near, 1.0, 0.0)
    n = tile.shape[1]
    before = jnp.where(iota((n, n), 0) < iota((n, n), 1), 1.0, 0.0)
    rank = jnp.dot(jnp.broadcast_to(mask, (ROWS, n)), before, preferred_element_type=F32)[:1]
    place = jnp.where(iota((n, n), 0) == rank.astype(jnp.int32), mask, 0.0)
    return mask, place


def pack_kernel(where_ref, pos_ref, burgers_ref, tile_ref, out_ref):
    mask, place = near_rank(tile_ref[...], where_ref[1])
    rest = jnp.broadcast_to(mask, (2, mask.shape[1]))
    segs = jnp.concatenate([pos_ref[...], burgers_ref[...], rest], axis=0)
    place = place.astype(BF16)
    place = jnp.concatenate([place, place, place], axis=1)
    packed = lax.dot_general(thirds(segs), place, NT, preferred_element_type=F32)
    out_ref[...] = jnp.broadcast_to(packed[None], out_ref.shape)


def measured(groups_ref):
    offset, longest = 0, 0
    places = []
    for r in range(groups_ref.shape[0]):
        count = jnp.sum(groups_ref[r, 6:7, :]).astype(jnp.int32)
        places.append((offset, count))
        offset = offset + count
        longest = jnp.maximum(longest, count)
    return places, offset, longest


def by_width(longest, width, run):
    half = width // 2

    @pl.when(longest <= half)
    def _():
        run(half)

    @pl.when(longest > half)
    def _():
        run(width)


def assemble(groups_ref, sbuf):
    places, total, longest = measured(groups_ref)

    def run(rows):
        for r, (offset, _) in enumerate(places):
            sbuf[pl.ds(offset, rows), 0:ROWS] = groups_ref[r].T[0:rows]

    by_width(longest, groups_ref.shape[2], run)
    sbuf[pl.ds(total, CHUNK), 0:ROWS] = jnp.zeros((CHUNK, ROWS), F32)
    return places, total, longest


def in_chunks(total, chunk):
    quarter, half = CHUNK // 4, CHUNK // 2
    whole = total // CHUNK
    rest = total - whole * CHUNK
    n = whole + jnp.where(rest > half, 1, 0)

    def step(i, carry):
        chunk(pl.multiple_of(i * CHUNK, CHUNK), CHUNK)
        return carry

    lax.fori_loop(0, n, step, jnp.int32(0))
    for least, most in ((0, quarter), (quarter, half)):

        @pl.when(jnp.logical_and(rest > least, rest <= most))
        def _():
            chunk(pl.multiple_of(whole * CHUNK, CHUNK), most)


def spread(sbuf, wide, start, size):
    for d in range(3):
        wide[d, 0:size] = jnp.broadcast_to(sbuf[pl.ds(start, size), d : d + 1], (size, LANES))


def cubes(wide, q_ref, start, size):
    his, los = [], []
    for j in range(CHUNK // LANES):
        at = pl.ds(pl.multiple_of(start + j * LANES, LANES), LANES)
        dx = wide[0, 0:size] - q_ref[0:1, at]
        dy = wide[1, 0:size] - q_ref[1:2, at]
        dz = wide[2, 0:size] - q_ref[2:3, at]
        inverse = lax.rsqrt((dx * dx + CORE) + (dy * dy + dz * dz))
        hi, lo = split(inverse * inverse * inverse)
        his.append(hi)
        los.append(lo)
    return jnp.concatenate(his, axis=1), jnp.concatenate(los, axis=1)


def traction_kernel(scale, groups_ref, q_ref, kq_ref, out_ref, sent_ref, kept_ref, sbuf, wide, total):
    q_dev = q_ref.shape[1]
    _, length, _ = assemble(groups_ref, sbuf)
    total[...] = jnp.zeros_like(total)

    def chunk(start, size):
        spread(sbuf, wide, start, size)
        vectors = jnp.concatenate(split(sbuf[pl.ds(start, size), 0:ROWS].T), axis=0)
        vectors = jnp.concatenate([vectors, vectors], axis=1)
        slot = jnp.minimum(start // CHUNK, KEPT)

        def block(j, c):
            at = pl.multiple_of(j * CHUNK, CHUNK)
            hi, lo = cubes(wide, q_ref, at, size)
            kept_ref[slot, 0, 0:size, pl.ds(at, CHUNK)] = hi
            kept_ref[slot, 1, 0:size, pl.ds(at, CHUNK)] = lo
            weights = jnp.concatenate([hi, lo], axis=0)
            total[:, pl.ds(at, CHUNK)] += jnp.dot(vectors, weights, preferred_element_type=F32)
            return c

        lax.fori_loop(0, q_dev // CHUNK, block, jnp.int32(0), unroll=8)

    in_chunks(length, chunk)
    both = (total[0:ROWS, :] + total[ROWS : 2 * ROWS, :]) * scale
    out_ref[...] = jnp.zeros_like(out_ref)
    out_ref[0:3, :] = both[3:6, :]
    half = q_dev // 2
    for p in range(2):
        at = slice(p * half, (p + 1) * half)
        sent_ref[4 * p : 4 * p + 3, :] = both[3:6, at]
        sent_ref[4 * p + 3 : 4 * p + 4, :] = kq_ref[0:1, at]


def nodes_of(nodes_ref, r, n):
    return nodes_ref[pl.ds(pl.multiple_of(r * n, n), n), :]


def set_hot(nodes, out_ref, first):
    rows = out_ref.shape[0]
    for k in range(nodes.shape[0]):
        row = nodes[k : k + 1, :] // LANES - first
        here = jnp.where(iota((rows, LANES), 0) == row, 1.0, 0.0)
        out_ref[:, k * LANES : (k + 1) * LANES] = here.astype(BF16)


def set_spot(nodes, out_ref):
    for k in range(nodes.shape[0]):
        here = jnp.where(iota((LANES, LANES), 0) == nodes[k : k + 1, :] % LANES, 1.0, 0.0)
        out_ref[:, k * LANES : (k + 1) * LANES] = here.astype(BF16)


def spread_points(spot_ref, values, cols):
    n = spot_ref.shape[1]
    for p, parts in enumerate(split(values)):
        for c in range(3):
            to = (p * 3 + c) * LANES
            for k in range(0, n, CHUNK):
                at = slice(k, k + CHUNK)
                part = jnp.broadcast_to(parts[c : c + 1, at], (LANES, CHUNK))
                cols[to : to + LANES, at] = spot_ref[:, at] * part


def layers(hot, cols):
    out = lax.dot_general(hot, cols, NT, preferred_element_type=F32)
    half = 3 * LANES
    return out[:, :half] + out[:, half:]


def set_parts(parts, place, x, rows, tile):
    hi, lo = split(tile)
    to = slice(place * LANES, (place + 1) * LANES)
    parts[to, x * LANES : (x + 1) * LANES] = hi
    parts[to, rows + x * LANES : rows + (x + 1) * LANES] = lo


def pair(nodes, k):
    return jnp.concatenate([nodes[k : k + 1, :], nodes[k + 1 : k + 2, :]], axis=1)


def gather(nodes, hot_ref, parts, fields, out_ref, first):
    for k in range(0, nodes.shape[0], 2):
        at = slice(k * LANES, (k + 2) * LANES)
        here = hot_ref[0 : parts.shape[1] // 2, at]
        found = jnp.dot(parts[...], jnp.concatenate([here, here], axis=0), preferred_element_type=F32)
        pick = iota((LANES, 2 * LANES), 0) == pair(nodes, k) % LANES
        for f in range(fields):
            value = jnp.where(pick, found[f * LANES : (f + 1) * LANES, :], 0.0)
            out_ref[first + f : first + f + 1, at] = jnp.sum(value, axis=0, keepdims=True)


def prepare_kernel(where_ref, nodes_ref, k_ref, kq_ref, kz_ref, hot_ref, parts):
    rows = k_ref.shape[0]
    n = kq_ref.shape[1] // LANES
    nodes = nodes_of(nodes_ref, where_ref[0], n)
    set_hot(nodes, hot_ref.at[0:rows], 0)
    set_spot(nodes, hot_ref.at[rows : rows + LANES])
    kz_ref[...] = jnp.zeros_like(kz_ref)
    for x in range(rows // LANES):
        at = slice(x * LANES, (x + 1) * LANES)
        tile = k_ref[at, :].T
        kz_ref[0:1, at] = tile[0:1, :]
        set_parts(parts, 0, x, rows, tile)
    kq_ref[...] = jnp.zeros_like(kq_ref)
    gather(nodes, hot_ref, parts, 1, kq_ref, 0)


def scatter_kernel(
    where_ref, nodes_ref, t_ref, hot_ref, b_ref, g_ref, low_ref, next_ref, high_ref, cols, parts
):
    n = t_ref.shape[1] // LANES
    rows = b_ref.shape[1]
    spread_points(hot_ref.at[rows : rows + LANES], t_ref[...], cols)
    load = layers(hot_ref[0:rows, :], cols[...])
    for ref in (low_ref, next_ref, high_ref):
        ref[...] = jnp.zeros_like(ref)
    for c in range(3):
        for x in range(rows // LANES):
            at = slice(x * LANES, (x + 1) * LANES)
            f = load[at, c * LANES : (c + 1) * LANES]
            b_ref[c, at, :] = f
            tile = f.T
            set_parts(parts, c, x, rows, tile)
            low_ref[c : c + 1, at] = tile[0:1, :]
            next_ref[c : c + 1, at] = tile[1:2, :]
            high_ref[c : c + 1, at] = tile[LANES - 1 : LANES, :]
    g_ref[...] = jnp.zeros_like(g_ref)
    gather(nodes_of(nodes_ref, where_ref[0], n), hot_ref, parts, 3, g_ref, 0)


def unfold(sent):
    return jnp.concatenate([sent[0:4], sent[4:8]], axis=1)


def sides_kernel(
    n_seg, where_ref, nodes_ref, left_ref, right_ref, low_ref, next_ref, high_ref, kz_ref,
    sides_ref, down_ref, up_ref, hot, spot, cols,
):
    n = hot.shape[1] // LANES
    rows = low_ref.shape[1]
    me = where_ref[0]
    down_ref[...] = jnp.zeros_like(down_ref)
    up_ref[...] = jnp.zeros_like(up_ref)
    own = slice(LANES, LANES + rows)
    down_ref[0:3, own] = low_ref[0:3, :]
    down_ref[3:6, own] = next_ref[0:3, :]
    down_ref[6:7, own] = kz_ref[0:1, :]
    up_ref[0:3, own] = high_ref[0:3, :]

    nodes = nodes_of(nodes_ref, jnp.maximum(me - 1, 0), n)
    set_hot(nodes, hot.at[0:LANES], rows - LANES)
    set_spot(nodes, spot)
    spread_points(spot, unfold(left_ref[...]) * jnp.where(me > 0, 1.0, 0.0), cols)
    left = layers(hot[0:LANES, :], cols[...])
    nodes = nodes_of(nodes_ref, jnp.minimum(me + 1, n_seg - 1), n)
    set_hot(nodes, hot, 0)
    set_spot(nodes, spot)
    t = unfold(right_ref[...])
    kq = t[3:4]
    t = t * jnp.where(me < n_seg - 1, 1.0, 0.0)
    spread_points(spot, t, cols)
    right = layers(hot[...], cols[...])
    spread_points(spot, t * kq, cols)
    stiff = layers(hot[0:LANES, :], cols[...])
    last = slice(LANES + rows, 2 * LANES + rows)
    for c in range(3):
        comp = slice(c * LANES, (c + 1) * LANES)
        sides_ref[c] = left[:, comp]
        sides_ref[3 + c] = right[0:LANES, comp]
        sides_ref[6 + c] = right[LANES : 2 * LANES, comp]
        sides_ref[9 + c] = stiff[:, comp]
        down_ref[c : c + 1, 0:LANES] = left[:, comp].T[0:1, :]
        tile = right[0:LANES, comp].T
        down_ref[c : c + 1, last] = tile[0:1, :]
        up_ref[c : c + 1, last] = tile[LANES - 1 : LANES, :]


def before_in_layer(f):
    i, j = iota(f.shape, 0), iota(f.shape, 1)
    return jnp.where(i == 0, 0.0, pltpu.roll(f, 1, 0)) + jnp.where(j == 0, 0.0, pltpu.roll(f, 1, 1))


def beside_in_layer(f):
    i, j = iota(f.shape, 0), iota(f.shape, 1)
    n, m = f.shape
    up = jnp.where(i == 0, 0.0, pltpu.roll(f, 1, 0)) + jnp.where(i == n - 1, 0.0, pltpu.roll(f, n - 1, 0))
    return up + (jnp.where(j == 0, 0.0, pltpu.roll(f, 1, 1)) + jnp.where(j == m - 1, 0.0, pltpu.roll(f, m - 1, 1)))


def operate_kernel(
    where_ref, nodes_ref, b_ref, sides_ref, k_ref, g_ref, hot_ref, u_ref, ur_ref, motion_ref, high_ref, parts
):
    n = g_ref.shape[1] // LANES
    rows = b_ref.shape[1]
    wide = rows // LANES
    high_ref[...] = jnp.zeros_like(high_ref)
    for c in range(3):
        b4 = sides_ref[3 + c]
        field = [sides_ref[c]] + [b_ref[c, x * LANES : (x + 1) * LANES, :] for x in range(wide)] + [b4]
        for x in range(wide):
            at = slice(x * LANES, (x + 1) * LANES)
            f = field[x + 1]
            u = (6.0 + k_ref[at, :]) * f - (beside_in_layer(f) + (field[x] + field[x + 2]))
            u_ref[c, at, :] = u
            tile = u.T
            high_ref[c : c + 1, at] = tile[LANES - 1 : LANES, :]
            set_parts(parts, c, x, rows, tile)
        ur_ref[c] = 6.0 * b4 + sides_ref[9 + c] - (field[wide] + sides_ref[6 + c] + beside_in_layer(b4))
    motion_ref[...] = g_ref[...]
    gather(nodes_of(nodes_ref, where_ref[0], n), hot_ref, parts, 3, motion_ref, 3)


def ends_kernel(
    n_seg, n_fe, where_ref, nodes_ref, b_ref, u_ref, ur_ref, k_ref, above_ref, below_ref, uh_ref, high_ref, g_ref,
    hot_ref, out_ref, motion_ref, sums_ref,
):
    n = g_ref.shape[1] // LANES
    rows = b_ref.shape[1]
    wide = rows // LANES
    me, block = where_ref[0], where_ref[1]
    is_above = jnp.where(block < n_fe - 1, 1.0, 0.0)
    above = above_ref[...] * is_above
    below = below_ref[...] * jnp.where(block > 0, 1.0, 0.0)
    own = slice(LANES, LANES + rows)

    center = above[0:3, own]
    place = iota(center.shape, 1) % LANES
    beside = above[0:3, 0:rows] + above[0:3, 2 * LANES : 2 * LANES + rows]
    beside = beside + jnp.where(place == 0, 0.0, pltpu.roll(center, 1, 1))
    beside = beside + jnp.where(place == LANES - 1, 0.0, pltpu.roll(center, rows - 1, 1))
    beside = beside + high_ref[0:3, :] + above[3:6, own]
    next_u = (6.0 + above[6:7, own]) * center - beside
    crossing = is_above * jnp.sum((uh_ref[0:3, :] - center) * next_u)

    above_t, below_t = above.T, below.T
    lane = iota((LANES, LANES), 1)
    zero = jnp.zeros((LANES, LANES), F32)
    bb, bu, uu, uau = zero, zero, zero, zero
    not_last = jnp.where(me < n_seg - 1, 1.0, 0.0)

    def ends(c, x):
        at = slice((x + 1) * LANES, (x + 2) * LANES)
        low = jnp.where(lane == 0, below_t[at, c : c + 1], 0.0)
        return low + jnp.where(lane == LANES - 1, above_t[at, c : c + 1], 0.0)

    for c in range(3):
        us = []
        for x in range(wide):
            at = slice(x * LANES, (x + 1) * LANES)
            f = b_ref[c, at, :]
            u = u_ref[c, at, :] - ends(c, x)
            out_ref[c, at, :] = u
            us.append(u)
            bb = bb + f * f
            bu = bu + f * u
            uu = uu + u * u
        us.append(not_last * (ur_ref[c] - ends(c, wide)))
        for x in range(wide):
            at = slice(x * LANES, (x + 1) * LANES)
            beside = before_in_layer(us[x]) + us[x + 1]
            uau = uau + us[x] * ((6.0 + k_ref[at, :]) * us[x] - 2.0 * beside)
    line = iota((1, LANES), 1)
    sums = jnp.where(line == 3, -2.0 * crossing, 0.0)
    for i, part in enumerate((bb, bu, uu, uau)):
        sums = sums + jnp.where(line == i, jnp.sum(part), 0.0)
    sums_ref[...] = jnp.broadcast_to(sums, sums_ref.shape)

    nodes = nodes_of(nodes_ref, me, n)
    faces = jnp.concatenate(split(below[:, own]) + split(above[:, own]), axis=0)
    motion_ref[...] = g_ref[...]
    for k in range(0, n, 2):
        at = slice(k * LANES, (k + 2) * LANES)
        found = jnp.dot(faces, hot_ref[0:rows, at], preferred_element_type=F32)
        last = pair(nodes, k) % LANES
        extra = jnp.where(last == 0, found[0:3] + found[8:11], 0.0)
        extra = extra + jnp.where(last == LANES - 1, found[16:19] + found[24:27], 0.0)
        motion_ref[3:6, at] = g_ref[3:6, at] - extra


def stress_kernel(groups_ref, kept_ref, q_ref, g_ref, sums_ref, out_ref, sbuf, wide, results, motion):
    q_dev = q_ref.shape[1]
    n_groups, _, width = out_ref.shape
    places, length, longest = measured(groups_ref)
    motion[...] = jnp.concatenate(split(g_ref[...]), axis=0)
    n_chunks = (length + (CHUNK - 1)) // CHUNK

    def from_kept(start, size):
        i = start // CHUNK
        m = motion[...]
        found = lax.dot_general(kept_ref[i, 0, 0:size], m, NT, preferred_element_type=F32)
        found = found + lax.dot_general(kept_ref[i, 1, 0:size], m, NT, preferred_element_type=F32)
        results[pl.ds(start, size), 0 : 2 * ROWS] = found

    in_chunks(jnp.minimum(length, KEPT * CHUNK), from_kept)

    def again(i, carry):
        start = pl.multiple_of(i * CHUNK, CHUNK)
        spread(sbuf, wide, start, CHUNK)

        def block(j, total):
            at = pl.multiple_of(j * CHUNK, CHUNK)
            hi, lo = cubes(wide, q_ref, at, CHUNK)
            m = motion[:, pl.ds(at, CHUNK)]
            total = total + lax.dot_general(hi, m, NT, preferred_element_type=F32)
            return total + lax.dot_general(lo, m, NT, preferred_element_type=F32)

        results[pl.ds(start, CHUNK), 0 : 2 * ROWS] = lax.fori_loop(
            0, q_dev // CHUNK, block, jnp.zeros((CHUNK, 2 * ROWS), F32), unroll=8
        )
        return carry

    @pl.when(n_chunks > KEPT)
    def _():
        assemble(groups_ref, sbuf)
        lax.fori_loop(KEPT, n_chunks, again, jnp.int32(0))

    def run(rows):
        row = iota((ROWS, rows), 0)
        for r, (offset, count) in enumerate(places):
            found = results[pl.ds(offset, rows), 0 : 2 * ROWS].T
            found = found[0:ROWS] + found[ROWS : 2 * ROWS]
            found = jnp.where(iota((ROWS, rows), 1) < count, found, 0.0)
            out_ref[r, :, 0:rows] = jnp.where(row == 6, sums_ref[:, 0:rows], found)
            if rows < width:
                out_ref[r, :, rows:width] = jnp.zeros((ROWS, width - rows), F32)

    by_width(longest, width, run)


def unpack_kernel(where_ref, tile_ref, partial_ref, out_ref):
    _, place = near_rank(tile_ref[...], where_ref[1])
    total = jnp.sum(partial_ref[...], axis=0)
    place = place.astype(BF16)
    place = jnp.concatenate([place, place, place], axis=0)
    spreaded = jnp.dot(thirds(total), place, preferred_element_type=F32)
    total = jnp.where(iota(total.shape, 0) == 6, total, spreaded)
    out_ref[...] = jnp.broadcast_to(total[None], out_ref.shape)


def finish_kernel(scale, partial_ref, b_ref, u_ref, correction_ref, stress_ref):
    total = jnp.sum(partial_ref[...], axis=0)
    bb, bu, uu, uau = [total[6:7, i : i + 1] for i in range(4)]
    alpha = bb / bu
    later = bb - 2.0 * alpha * bu + alpha * alpha * uu
    beta = later / bb
    grow = 1.0 + beta
    alpha_next = later / (grow * grow * bu - 2.0 * alpha * grow * uu + alpha * alpha * uau)
    on_b = alpha + alpha_next * grow
    on_u = -alpha_next * alpha
    stress_ref[...] = (on_b * total[0:3] + on_u * total[3:6]) * scale
    for c in range(3):
        correction_ref[c] = on_b * b_ref[c] + on_u * u_ref[c]


def call(kernel, out, scratch=(), placed=False, inputs=0, flops=0, moved=0, limit=VMEM_LIMIT):
    vmem = pl.BlockSpec(memory_space=pltpu.VMEM)
    shapes = []
    for o in out:
        shapes.append(o if isinstance(o, jax.ShapeDtypeStruct) else jax.ShapeDtypeStruct(o, F32))
    single = len(shapes) == 1

    def with_place(*refs):
        kernel((lax.axis_index("seg"), lax.axis_index("fe")), *refs)

    return pl.pallas_call(
        with_place if placed else kernel,
        out_shape=shapes[0] if single else tuple(shapes),
        in_specs=[vmem] * inputs,
        out_specs=vmem if single else (vmem,) * len(shapes),
        scratch_shapes=list(scratch),
        compiler_params=pltpu.CompilerParams(vmem_limit_bytes=limit),
        cost_estimate=pl.CostEstimate(flops=flops, bytes_accessed=moved, transcendentals=0),
    )


def shards(seg_pos, burgers, seg_tile, quad_pos, quad_node, stiffness):
    n_seg, n_fe = lax.axis_size("seg"), lax.axis_size("fe")
    column = lax.axis_index("seg")
    s_dev = seg_pos.shape[1]
    q_block = quad_pos.shape[1]
    q_dev = q_block // n_seg
    total_segs = s_dev * n_seg
    total_points = q_block * n_fe
    wide, tall, deep = stiffness.shape
    rows = wide * tall
    tile = seg_tile.reshape(1, s_dev)
    nodes = quad_node.reshape(q_block // LANES, LANES)
    points = lax.dynamic_slice_in_dim(quad_pos, column * q_dev, q_dev, 1)
    stiff = stiffness.reshape(rows, deep)

    up_seg = [(i, (i + 1) % n_seg) for i in range(n_seg)]
    down_seg = [((i + 1) % n_seg, i) for i in range(n_seg)]
    up_fe = [(i, (i + 1) % n_fe) for i in range(n_fe)]
    down_fe = [((i + 1) % n_fe, i) for i in range(n_fe)]
    field, line = (3, rows, deep), (ROWS, q_dev)
    face, message = (ROWS, rows), (ROWS, rows + 2 * LANES)
    long = total_segs + 2 * CHUNK
    sbuf = pltpu.VMEM((long, LANES), F32)
    spreaded = pltpu.VMEM((3, CHUNK, LANES), F32)
    cols = pltpu.VMEM((6 * LANES, q_dev), BF16)

    packed = call(
        pack_kernel, [(n_seg, ROWS, s_dev)], placed=True, inputs=3, limit=PACK_LIMIT
    )(seg_pos, burgers, tile)
    groups = lax.all_to_all(packed, "seg", 0, 0, tiled=True)
    kq, kz, hot = call(
        prepare_kernel, [line, face, jax.ShapeDtypeStruct((rows + LANES, q_dev), BF16)],
        [pltpu.VMEM((LANES, 2 * rows), BF16)], placed=True, inputs=2, flops=10**9, moved=10**6, limit=PACK_LIMIT,
    )(nodes, stiff)

    def traction(*refs):
        traction_kernel(STRENGTH / math.sqrt(total_segs), *refs)

    weights = jax.ShapeDtypeStruct((KEPT + 1, 2, CHUNK, q_dev), BF16)
    t, sent, kept = call(
        traction, [line, (ROWS, q_dev // 2), weights], [sbuf, spreaded, pltpu.VMEM((2 * ROWS, q_dev), F32)], inputs=3,
        flops=10**10, moved=10**6,
    )(groups, points, kq[0:1])
    from_left = lax.ppermute(sent, "seg", up_seg)
    from_right = lax.ppermute(sent, "seg", down_seg)

    b, g, low, after, high = call(
        scatter_kernel, [field, line, face, face, face], [cols, pltpu.VMEM((3 * LANES, 2 * rows), BF16)],
        placed=True, inputs=3, flops=4 * 10**9, moved=4 * 10**6,
    )(nodes, t, hot)

    def fill_sides(*refs):
        sides_kernel(n_seg, *refs)

    sides, down, up = call(
        fill_sides, [(12, tall, deep), message, message],
        [pltpu.VMEM((2 * LANES, q_dev), BF16), pltpu.VMEM((LANES, q_dev), BF16), cols],
        placed=True, inputs=7, flops=2 * 10**9, moved=10**6,
    )(nodes, from_left, from_right, low, after, high, kz)
    above = lax.ppermute(down, "fe", down_fe)
    below = lax.ppermute(up, "fe", up_fe)
    u, ur, g, uh = call(
        operate_kernel, [field, (3, tall, deep), line, face], [pltpu.VMEM((3 * LANES, 2 * rows), BF16)],
        placed=True, inputs=6, flops=4 * 10**9, moved=4 * 10**6,
    )(nodes, b, sides, stiff, g, hot)

    def fill_ends(*refs):
        ends_kernel(n_seg, n_fe, *refs)

    u, motion, sums = call(
        fill_ends, [field, line, (ROWS, LANES)], placed=True, inputs=11, flops=10**9, moved=4 * 10**6
    )(nodes, b, u, ur, stiff, above, below, uh, high, g, hot)
    partial = call(
        stress_kernel, [(n_seg, ROWS, s_dev)],
        [sbuf, spreaded, pltpu.VMEM((long, LANES), F32), pltpu.VMEM((2 * ROWS, q_dev), BF16)],
        inputs=5, flops=10**10, moved=10**6,
    )(groups, kept, points, motion, sums)
    partial = lax.all_to_all(partial, "seg", 0, 0, tiled=True)
    partial = call(unpack_kernel, [(n_fe, ROWS, s_dev)], placed=True, inputs=2)(tile, partial)
    partial = lax.all_to_all(partial, "fe", 0, 0, tiled=True)

    def finish(*refs):
        finish_kernel(4.0 * STRENGTH / math.sqrt(total_points), *refs)

    correction, stress = call(finish, [(3, rows, deep), (3, s_dev)], inputs=3)(partial, b, u)
    return correction.reshape(3, wide, tall, deep), stress


def solution(mesh):
    placed = (
        P(None, "seg"),
        P(None, "seg"),
        P("seg"),
        P(None, "fe"),
        P("fe"),
        P("seg", None, "fe"),
    )
    return jax.shard_map(
        shards,
        mesh=mesh,
        in_specs=placed,
        out_specs=(P(None, "seg", None, "fe"), P(None, "seg")),
        check_vma=False,
    )
```
